128 devices in a mesh: row: 8 (over y, z_lo), col: 16 (over z_hi, x, core).
Axes of the slice: x: 4, y: 4, z: 4 (z_hi: 2, z_lo: 2; z = z_hi * 2 + z_lo), core: 2. Of those that a mesh axis runs over, the one named last changes fastest.
Arguments:
- data: bfloat16 [8, 16, 32, 1024, 128], P('row', 'col'), may hold values from -6 to 6
- real_index: int32 [8, 16, 2, 2], P('row', 'col'), may hold values from 0 to 31
- latent_seed: int32 [8, 16, 2, 2], P('row', 'col'), may hold values from 0 to 255
- latent_bank: float32 [256, 128], replicated, may hold values from -6 to 6
- g_in: float32 [8, 16, 128, 128], P('row', 'col'), may hold values from -0.5 to 0.5
- g_base: float32 [8, 16, 1024, 128], P('row', 'col'), may hold values from -6 to 6
- g_one: float32 [8, 16, 128, 128], P('row', 'col'), may hold values from -0.5 to 0.5
- g_two: float32 [8, 16, 128, 128], P('row', 'col'), may hold values from -0.5 to 0.5
- d_one: float32 [8, 16, 128, 128], P('row', 'col'), may hold values from -0.5 to 0.5
- d_two: float32 [8, 16, 128, 128], P('row', 'col'), may hold values from -0.5 to 0.5
- d_out: float32 [8, 16, 128], P('row', 'col'), may hold values from -0.5 to 0.5
Outputs:
- new_g_in: float32 [8, 16, 128, 128], P('row', 'col')
- new_g_base: float32 [8, 16, 1024, 128], P('row', 'col')
- new_g_one: float32 [8, 16, 128, 128], P('row', 'col')
- new_g_two: float32 [8, 16, 128, 128], P('row', 'col')
- new_d_one: float32 [8, 16, 128, 128], P('row', 'col')
- new_d_two: float32 [8, 16, 128, 128], P('row', 'col')
- new_d_out: float32 [8, 16, 128], P('row', 'col')
- verdicts: float32 [8, 16, 2, 12], P('row', 'col')
The draws below stay inside these ranges and needn't reach their ends.
All inputs are finite; a program needn't handle non-finite values.
Results may differ from the reference program's by a relative error of at most 0.0028.
Values may be sent and summed in bfloat16 or wider, within the bound.
No kernel may reach another device: no remote copies, remote signals or barrier semaphores. Data moves between devices by JAX's collectives and lax.ppermute only.
A program may use at most 128 MiB of HBM per device.

```python
import jax
import jax.numpy as jnp
from jax import lax

POSITIONS = 1024
CHANNELS = 128
LATENT = 128
FAKES = 2
REALS = 2
DATA = 32
BANK = 256
STEPS = 2
GRID_ROWS = 8
GRID_COLS = 16


def set_ends(array, rng, low, high):
    dims = array.shape
    spot = [jax.random.randint(jax.random.fold_in(rng, axis), (), 0, dims[axis]) for axis in range(len(dims))]
    array = array.at[tuple(spot)].set(low)
    longest = dims.index(max(dims))
    spot[longest] = (spot[longest] + 1) % dims[longest]
    return array.at[tuple(spot)].set(high)


def level_of(stream_key, shape, cuts, low, top_value):
    factor_of = 1.0
    for position, shards_of in cuts:
        steps = jax.random.uniform(jax.random.fold_in(jax.random.fold_in(stream_key, 6), position), (shards_of,), jnp.float32, low / len(cuts), top_value / len(cuts))
        factor_of = factor_of * jnp.repeat(jnp.exp(steps), shape[position] // shards_of).reshape((-1,) + (1,) * (len(shape) - 1 - position))
    return factor_of


def scatter_about(stream_key, extent, deviation, most, split=(), kind=jnp.bfloat16):
    factor_of = level_of(stream_key, extent, split, -0.22, 0.18) if split else 1.0
    values = jax.random.normal(stream_key, extent, jnp.float32) * deviation * factor_of
    return jnp.minimum(jnp.maximum(values, -most), most).astype(kind)


def setup_inputs(seed: int = 0) -> dict:
    streams_of = jax.random.split(jax.random.key(seed), 12)
    return {
        "data": scatter_about(streams_of[0], (GRID_ROWS, GRID_COLS, DATA, POSITIONS, CHANNELS), 1.0, 6.0, ((0, 8), (1, 16))),
        "real_index": set_ends(jax.random.randint(streams_of[1], (GRID_ROWS, GRID_COLS, STEPS, REALS), 0, DATA), jax.random.fold_in(streams_of[1], 1), 0, DATA - 1).astype(jnp.int32),
        "latent_seed": set_ends(jax.random.randint(streams_of[2], (GRID_ROWS, GRID_COLS, STEPS, FAKES), 0, BANK), jax.random.fold_in(streams_of[2], 1), 0, BANK - 1).astype(jnp.int32),
        "latent_bank": scatter_about(streams_of[3], (BANK, LATENT), 1.0, 6.0, (), jnp.float32),
        "g_in": scatter_about(streams_of[4], (GRID_ROWS, GRID_COLS, LATENT, CHANNELS), LATENT ** -0.5, 0.5, ((0, 8), (1, 16)), jnp.float32),
        "g_base": scatter_about(streams_of[5], (GRID_ROWS, GRID_COLS, POSITIONS, CHANNELS), 1.0, 6.0, ((0, 8), (1, 16)), jnp.float32),
        "g_one": scatter_about(streams_of[6], (GRID_ROWS, GRID_COLS, CHANNELS, CHANNELS), CHANNELS ** -0.5, 0.5, ((0, 8), (1, 16)), jnp.float32),
        "g_two": scatter_about(streams_of[7], (GRID_ROWS, GRID_COLS, CHANNELS, CHANNELS), CHANNELS ** -0.5, 0.5, ((0, 8), (1, 16)), jnp.float32),
        "d_one": scatter_about(streams_of[8], (GRID_ROWS, GRID_COLS, CHANNELS, CHANNELS), CHANNELS ** -0.5, 0.5, ((0, 8), (1, 16)), jnp.float32),
        "d_two": scatter_about(streams_of[9], (GRID_ROWS, GRID_COLS, CHANNELS, CHANNELS), CHANNELS ** -0.5, 0.5, ((0, 8), (1, 16)), jnp.float32),
        "d_out": scatter_about(streams_of[10], (GRID_ROWS, GRID_COLS, CHANNELS), CHANNELS ** -0.5, 0.5, ((0, 8), (1, 16)), jnp.float32),
    }


learn_rate = 0.05
base_rate = 0.1


def matmul(left_side, right_side):
    return jnp.dot(left_side.astype(jnp.float32), right_side.astype(jnp.float32), preferred_element_type=jnp.float32)


def rows_matmul(left_side, right_side):
    return lax.dot_general(left_side.astype(jnp.float32), right_side.astype(jnp.float32), (((0,), (0,)), ((), ())), preferred_element_type=jnp.float32)


def silu_slope(values):
    sigmoid_part = jax.nn.sigmoid(values)
    return sigmoid_part * (1.0 + values * (1.0 - sigmoid_part))


def generate(latent, weights):
    w_in, w_base, w_one, w_two = weights
    shifted = matmul(latent, w_in)
    batch_count = latent.shape[0]
    places, channels = w_base.shape
    gen_pre = (w_base.astype(jnp.float32)[None] + shifted[:, None, :]).reshape(batch_count * places, channels)
    hidden = jax.nn.silu(gen_pre).astype(jnp.bfloat16)
    middle_pre = matmul(hidden, w_one)
    middle = jax.nn.silu(middle_pre).astype(jnp.bfloat16)
    own_fakes = (lax.optimization_barrier(hidden).astype(jnp.float32) + matmul(middle, w_two)).astype(jnp.bfloat16)
    return own_fakes, (gen_pre, hidden, middle_pre, middle)


def generator_grads(cotangent, stored, latent, weights):
    gen_pre, hidden, middle_pre, middle = stored
    w_in, w_base, w_one, w_two = weights
    repeats = cotangent.shape[0] // hidden.shape[0]
    grad_two = rows_matmul(jnp.tile(middle, (repeats, 1)), cotangent)
    inner_term = matmul(cotangent, w_two.T) * jnp.tile(silu_slope(middle_pre), (repeats, 1))
    inner_half = inner_term.astype(jnp.bfloat16)
    grad_one = rows_matmul(jnp.tile(hidden, (repeats, 1)), inner_half)
    outer_term = (cotangent.astype(jnp.float32) + matmul(inner_half, w_one.T)) * jnp.tile(silu_slope(gen_pre), (repeats, 1))
    batch_count = latent.shape[0]
    places, channels = w_base.shape
    outer_term = outer_term.reshape(repeats, batch_count, places, channels)
    grad_base = jnp.sum(outer_term, axis=(0, 1))
    grad_in = jnp.dot(latent.astype(jnp.float32).T, jnp.sum(outer_term, axis=(0, 2)), precision=lax.Precision.HIGHEST)
    return grad_in, grad_base, grad_one, grad_two


def judge(images, d_one, d_two, d_out, batch_count):
    places = images.shape[0] // batch_count
    first_pre = matmul(images, d_one)
    first_act = jax.nn.silu(first_pre).astype(jnp.bfloat16)
    summed = images.astype(jnp.float32) + matmul(first_act, d_two)
    feature = jax.nn.silu(summed)
    verdict = jnp.sum(feature * d_out[None, :], axis=1).reshape(batch_count, places).mean(axis=1)
    return verdict, (first_pre, first_act, summed, feature)


def judge_back(slopes, stored, d_two, d_out, places):
    first_pre, first_act, summed, feature = stored
    weight_rows = jnp.repeat(slopes / places, places)
    outer_term = weight_rows[:, None] * d_out[None, :] * silu_slope(summed)
    outer_half = outer_term.astype(jnp.bfloat16)
    inner_half = (matmul(outer_half, d_two.T) * silu_slope(first_pre)).astype(jnp.bfloat16)
    return weight_rows, outer_term, outer_half, inner_half


def judge_cell_math(images, d_half, d_out, batch_count, fake_count, places):
    d_one, d_two = d_half
    verdict, stored = judge(images, d_one, d_two, d_out, batch_count)
    fake_verdict = verdict[:fake_count]
    real_verdict = verdict[fake_count:]
    disc_slope = jnp.concatenate([jax.nn.sigmoid(fake_verdict), -jax.nn.sigmoid(-real_verdict)])
    weight_rows, outer_term, outer_half, inner_half = judge_back(disc_slope, stored, d_two, d_out, places)
    grad_out = jnp.sum(stored[3] * weight_rows[:, None], axis=0)
    grad_two = rows_matmul(stored[1], outer_half)
    grad_one = rows_matmul(images, inner_half)
    fake_rows = fake_count * places
    fake_stored = tuple(member[:fake_rows] for member in stored)
    gen_slope = -jax.nn.sigmoid(-fake_verdict)
    unused, gen_outer, gen_half, gen_inner = judge_back(gen_slope, fake_stored, d_two, d_out, places)
    returned = (gen_outer + matmul(gen_inner, d_one.T)).astype(jnp.bfloat16)
    return verdict, (grad_one, grad_two, grad_out), returned


def reference(data, real_index, latent_seed, latent_bank, g_in, g_base, g_one, g_two, d_one, d_two, d_out):
    grid_rows = data.shape[0]
    grid_cols = data.shape[1]
    cells = grid_rows * grid_cols
    places = data.shape[3]
    channels = data.shape[4]
    batch_count = latent_seed.shape[3]
    reals_count = real_index.shape[3]
    fake_count = 5 * batch_count
    step_sizes = [learn_rate, base_rate * places, learn_rate, learn_rate, learn_rate, learn_rate, learn_rate]
    data_flat = data.reshape((cells,) + data.shape[2:])
    real_flat = real_index.reshape(cells, STEPS, reals_count)
    seed_flat = latent_seed.reshape(cells, STEPS, batch_count)
    params = [member.reshape((cells,) + member.shape[2:]) for member in (g_in, g_base, g_one, g_two, d_one, d_two, d_out)]
    bank_half = latent_bank.astype(jnp.bfloat16)
    cell_ids = jnp.arange(cells).astype(jnp.int32)
    rows_of = cell_ids // grid_cols
    cols_of = cell_ids % grid_cols
    north = ((rows_of - 1) % grid_rows) * grid_cols + cols_of
    south = ((rows_of + 1) % grid_rows) * grid_cols + cols_of
    west = rows_of * grid_cols + (cols_of - 1) % grid_cols
    east = rows_of * grid_cols + (cols_of + 1) % grid_cols
    neighbour_ids = jnp.stack([cell_ids, north, south, west, east], axis=1).astype(jnp.int32)
    verdict_list = []
    for step_index in range(STEPS):
        latents = bank_half[seed_flat[:, step_index]]
        halves = [member.astype(jnp.bfloat16) for member in params[:6]]

        def make_fakes(cell):
            return generate(latents[cell], tuple(member[cell] for member in halves[:4]))[0]

        all_fakes = lax.map(make_fakes, cell_ids)

        def judge_cell(cell):
            chosen = neighbour_ids[cell]
            judged = all_fakes[chosen].reshape(fake_count * places, channels)
            real_rows = data_flat[cell][real_flat[cell, step_index]].reshape(reals_count * places, channels)
            images = jnp.concatenate([judged, real_rows], axis=0)
            verdict, grads, returned = judge_cell_math(images, (halves[4][cell], halves[5][cell]), params[6][cell], fake_count + reals_count, fake_count, places)
            return verdict, grads, returned.reshape(5, batch_count * places, channels)

        verdict_all, disc_grads, returned_all = lax.map(judge_cell, cell_ids)

        def gen_cell(cell):
            chosen = neighbour_ids[cell]
            incoming = jnp.concatenate([returned_all[cell, 0], returned_all[chosen[1], 2], returned_all[chosen[2], 1], returned_all[chosen[3], 4], returned_all[chosen[4], 3]], axis=0)
            weights = tuple(member[cell] for member in halves[:4])
            own_fakes, stored = generate(latents[cell], weights)
            return generator_grads(incoming, stored, latents[cell], weights)

        gen_grads = lax.map(gen_cell, cell_ids)
        all_grads = list(gen_grads) + list(disc_grads)
        params = [member - step_size * grad for member, grad, step_size in zip(params, all_grads, step_sizes)]
        verdict_list.append(verdict_all)
    verdicts = jnp.stack(verdict_list, axis=1).reshape(grid_rows, grid_cols, STEPS, fake_count + reals_count)
    finals = [member.reshape((grid_rows, grid_cols) + member.shape[1:]) for member in params]
    return finals[0], finals[1], finals[2], finals[3], finals[4], finals[5], finals[6], verdicts
```

```python
import functools

import jax
import jax.numpy as jnp
from jax import lax
from jax.experimental import pallas as pl
from jax.experimental.pallas import tpu as pltpu
from jax.sharding import PartitionSpec as P

STEPS = 2
LEARN_RATE = 0.05
BASE_RATE = 0.1
PACKET = 272
HEAD = 256
VMEM_LIMIT = 24 * 1024 * 1024
F32 = jnp.float32
BF16 = jnp.bfloat16


def dot(left, right):
    return jnp.dot(left, right, preferred_element_type=F32)


def dot_rows(left, right):
    return lax.dot_general(left, right, (((0,), (0,)), ((), ())), preferred_element_type=F32)


def silu_parts(half):
    tanh_part = jnp.tanh(half)
    above = 1.0 + tanh_part
    value = half * above
    slope_twice = above + value * (1.0 - tanh_part)
    return value, slope_twice


def sigmoid(value):
    return 0.5 * (1.0 + jnp.tanh(0.5 * value))


def col_sums(tile):
    rows, channels = tile.shape
    return jnp.sum(tile.reshape(rows // 8, 8, channels), axis=0)


def split_two(value):
    high = value.astype(BF16)
    low = (value - high.astype(F32)).astype(BF16)
    return high, low


def call(body, out_shape, scratch=(), n_inputs=0, smem=(), **kwargs):
    in_specs = [
        pl.BlockSpec(memory_space=pltpu.SMEM if i in smem else pltpu.VMEM) for i in range(n_inputs)
    ]
    out_specs = [pl.BlockSpec(memory_space=pltpu.VMEM) for _ in out_shape]
    return pl.pallas_call(
        body,
        out_shape=tuple(out_shape),
        in_specs=in_specs,
        out_specs=tuple(out_specs),
        scratch_shapes=list(scratch),
        compiler_params=pltpu.CompilerParams(vmem_limit_bytes=VMEM_LIMIT),
        **kwargs,
    )


def shape(dims, dtype):
    return jax.ShapeDtypeStruct(dims, dtype)


def write_packet(packet_ref, one, two, out_row):
    channels = one.shape[0]
    packet_ref[0:channels, :] = one.astype(BF16)
    packet_ref[channels : 2 * channels, :] = two.astype(BF16)
    high, low = split_two(out_row)
    rest = PACKET - 2 * channels
    spot = lax.broadcasted_iota(jnp.int32, (rest, channels), 0)
    tail = jnp.where(spot == 0, high.astype(F32), jnp.where(spot == 1, low.astype(F32), 0.0))
    packet_ref[2 * channels : PACKET, :] = tail.astype(BF16)


def pack_body(one_ref, two_ref, out_ref, packet_ref):
    write_packet(packet_ref, one_ref[...], two_ref[...], out_ref[...])


def pack(d_one, d_two, d_out):
    return call(pack_body, [shape((PACKET, 128), BF16)], n_inputs=3)(d_one, d_two, d_out)[0]


def judge_tile(image, halves, weights):
    one_half, two_half, one_turned, two_half_turned, out_half = weights
    first, slope_first = silu_parts(dot(image, one_half))
    first_half = first.astype(BF16)
    feature, slope_out = silu_parts(halves + dot(first_half, two_half))
    outer = out_half * slope_out
    outer_half = outer.astype(BF16)
    inner_half = (dot(outer_half, two_half_turned) * slope_first).astype(BF16)
    unit = outer + dot(inner_half, one_turned)
    return first_half, feature, outer_half, inner_half, unit


def judge_body(fakes, reals, tile, *refs):
    refs = list(refs)
    index_ref = refs.pop(0) if reals else None
    packet_ref = refs.pop(0)
    fakes_ref = refs.pop(0)
    data_ref = refs.pop(0) if reals else None
    grads_ref, unit_ref, slope_ref = refs[:3]
    one_half, two_half, one_turned, two_turned, sum_one, sum_two, sum_out = refs[3:10]
    if reals:
        real_buf, real_sem = refs[10:12]
        copies = [
            pltpu.make_async_copy(data_ref.at[index_ref[i]], real_buf.at[i], real_sem.at[i])
            for i in range(reals)
        ]
        for copy in copies:
            copy.start()
    images = fakes + reals
    places = unit_ref.shape[1]
    channels = unit_ref.shape[2]

    one = packet_ref[0:channels, :].astype(F32)
    two = packet_ref[channels : 2 * channels, :].astype(F32)
    tail = packet_ref[2 * channels : PACKET, :].astype(F32)
    out_row = tail[0:1, :] + tail[1:2, :]
    one_half[...] = (0.5 * one).astype(BF16)
    two_half[...] = (0.5 * two).astype(BF16)
    one_turned[...] = one.T.astype(BF16)
    two_turned[...] = (0.5 * two).T.astype(BF16)
    sum_one[...] = jnp.zeros_like(sum_one)
    sum_two[...] = jnp.zeros_like(sum_two)
    sum_out[...] = jnp.zeros_like(sum_out)
    out_half = 0.5 * out_row

    def run(members, source, with_unit):
        def step(number, carry):
            rows = pl.ds(pl.multiple_of(number * tile, tile), tile)
            weights = (one_half[...], two_half[...], one_turned[...], two_turned[...], out_half)
            for member in members:
                image = source(member, rows)
                halves = 0.5 * image.astype(F32)
                first_half, feature, outer_half, inner_half, unit = judge_tile(image, halves, weights)
                if with_unit:
                    unit_ref[member, rows, :] = unit.astype(BF16)
                sum_out[member] += col_sums(feature)
                sum_two[member] += dot_rows(first_half, outer_half)
                sum_one[member] += dot_rows(image, inner_half)
            return carry

        lax.fori_loop(0, places // tile, step, 0)

    run(list(range(fakes)), lambda member, rows: fakes_ref[member, rows, :], True)
    if reals:
        for copy in copies:
            copy.wait()
        run(list(range(fakes, images)), lambda member, rows: real_buf[member - fakes, rows, :], False)

    total_one = jnp.zeros((channels, channels), F32)
    total_two = jnp.zeros((channels, channels), F32)
    total_out = jnp.zeros((1, channels), F32)
    scale = 1.0 / places
    verdict_rows = []
    for member in range(images):
        feature_sum = jnp.sum(sum_out[member], axis=0, keepdims=True)
        verdict = jnp.sum(feature_sum * out_row, axis=1, keepdims=True) * scale
        verdict = jnp.broadcast_to(verdict, (1, channels))
        verdict_rows.append(verdict)
        minus = -sigmoid(-verdict)
        slope = sigmoid(verdict) if member < fakes else minus
        slope = slope * scale
        if member < fakes:
            slope_ref[member : member + 1, :] = minus * scale
        total_one = total_one + slope * sum_one[member]
        total_two = total_two + slope * sum_two[member]
        total_out = total_out + slope * feature_sum
    if reals:
        grads_ref[0:channels, :] = total_one
        grads_ref[channels : 2 * channels, :] = total_two
        grads_ref[HEAD : HEAD + 1, :] = total_out
        for member in range(images):
            grads_ref[HEAD + 1 + member : HEAD + 2 + member, :] = verdict_rows[member]
    else:
        write_packet(grads_ref, total_one, total_two, total_out)
        rows = []
        for member in range(images):
            rows.extend(split_two(verdict_rows[member]))
        high, low = split_two(total_out)
        rows = [high, low] + rows
        spot = lax.broadcasted_iota(jnp.int32, (PACKET - HEAD, channels), 0)
        tail_rows = jnp.zeros((PACKET - HEAD, channels), F32)
        for place, row in enumerate(rows):
            tail_rows = jnp.where(spot == place, row.astype(F32), tail_rows)
        grads_ref[HEAD:PACKET, :] = tail_rows.astype(BF16)


def judge(packet, fakes, data=None, index=None, tile=256):
    fake_count, places, channels = fakes.shape
    reals = 0 if index is None else index.shape[0]
    square = (channels, channels)
    images = fake_count + reals
    scratch = [pltpu.VMEM(square, BF16)] * 4 + [
        pltpu.VMEM((images,) + square, F32),
        pltpu.VMEM((images,) + square, F32),
        pltpu.VMEM((images, 8, channels), F32),
    ]
    outs = [
        shape((PACKET, channels), F32 if reals else BF16),
        shape((fake_count, places, channels), BF16),
        shape((8, channels), F32),
    ]
    body = functools.partial(judge_body, fake_count, reals, tile)
    vmem = pl.BlockSpec(memory_space=pltpu.VMEM)
    if reals:
        scratch = scratch + [
            pltpu.VMEM((reals, places, channels), BF16),
            pltpu.SemaphoreType.DMA((reals,)),
        ]
        in_specs = [pl.BlockSpec(memory_space=pltpu.SMEM), vmem, vmem, pl.BlockSpec(memory_space=pl.ANY)]
        operands = (index, packet, fakes, data)
    else:
        in_specs = [vmem, vmem]
        operands = (packet, fakes)
    flops = images * places * channels * channels * 12
    return pl.pallas_call(
        body,
        out_shape=tuple(outs),
        in_specs=in_specs,
        out_specs=(vmem,) * 3,
        scratch_shapes=scratch,
        compiler_params=pltpu.CompilerParams(vmem_limit_bytes=VMEM_LIMIT),
        cost_estimate=pl.CostEstimate(flops=flops, bytes_accessed=2 * 1024 * 1024, transcendentals=0),
    )(*operands)


def gen_forward(seeds, bank_ref, w_in, base_ref, w_one, w_two, outs, tile):
    fakes_ref, hidden_ref, middle_ref, gen_slope_ref, mid_slope_ref, latent_ref = outs
    places, channels = base_ref.shape
    batch = len(seeds)
    latent_ref[...] = jnp.zeros_like(latent_ref)
    for member, seed in enumerate(seeds):
        latent_ref[member : member + 1, :] = (
            bank_ref[pl.ds(seed, 1), :].astype(BF16).astype(F32)
        )
    shifted = dot(latent_ref[...].astype(BF16), w_in.astype(BF16)) * 0.5
    one_half = (0.5 * w_one).astype(BF16)
    two = w_two.astype(BF16)

    def step(number, carry):
        rows = pl.ds(pl.multiple_of(number * tile, tile), tile)
        base = 0.5 * base_ref[rows, :].astype(BF16).astype(F32)
        for member in range(batch):
            hidden, slope_gen = silu_parts(base + shifted[member : member + 1, :])
            hidden_half = hidden.astype(BF16)
            middle, slope_mid = silu_parts(dot(hidden_half, one_half))
            middle_half = middle.astype(BF16)
            fake = hidden_half.astype(F32) + dot(middle_half, two)
            fakes_ref[member, rows, :] = fake.astype(BF16)
            hidden_ref[member, rows, :] = hidden_half
            middle_ref[member, rows, :] = middle_half
            gen_slope_ref[member, rows, :] = slope_gen
            mid_slope_ref[member, rows, :] = slope_mid
        return carry

    lax.fori_loop(0, places // tile, step, 0)


def gen_body(which, tile, seed_ref, bank_ref, in_ref, base_ref, one_ref, two_ref, *outs):
    seeds = [seed_ref[which, member] for member in range(seed_ref.shape[1])]
    gen_forward(seeds, bank_ref, in_ref[...], base_ref, one_ref[...], two_ref[...], outs, tile)


def stored_shapes(batch, places, channels):
    whole = (batch, places, channels)
    return [
        shape(whole, BF16),
        shape(whole, BF16),
        shape(whole, BF16),
        shape(whole, F32),
        shape(whole, F32),
        shape((8, channels), F32),
    ]


def generate(seed, which, bank, weights, tile=256):
    places, channels = weights[1].shape
    outs = stored_shapes(seed.shape[1], places, channels)
    return call(functools.partial(gen_body, which, tile), outs, n_inputs=6, smem=(0,))(
        seed, bank, *weights
    )


def gen_back_body(which, tile, judges, batch, *refs):
    refs = list(refs)
    units = [refs.pop(0) for _ in range(judges)]
    slopes = [refs.pop(0) for _ in range(judges)]
    hidden_ref, middle_ref, gen_slope_ref, mid_slope_ref, latent_ref = [refs.pop(0) for _ in range(5)]
    in_ref, base_ref, one_ref, two_ref = [refs.pop(0) for _ in range(4)]
    if which is not None:
        seed_ref, bank_ref = [refs.pop(0) for _ in range(2)]
    new_in, new_base, new_one, new_two = [refs.pop(0) for _ in range(4)]
    nexts = [refs.pop(0) for _ in range(6)] if which is not None else None
    one_turned, two_turned, sum_one, sum_two, sum_rows = refs
    places, channels = base_ref.shape
    base_step = BASE_RATE * places * 0.5

    one_turned[...] = one_ref[...].T.astype(BF16)
    two_turned[...] = (0.5 * two_ref[...]).T.astype(BF16)
    sum_one[...] = jnp.zeros_like(sum_one)
    sum_two[...] = jnp.zeros_like(sum_two)
    sum_rows[...] = jnp.zeros_like(sum_rows)

    def step(number, carry):
        rows = pl.ds(pl.multiple_of(number * tile, tile), tile)
        total = None
        for member in range(batch):
            cotangent = None
            for unit_ref, slope_ref in zip(units, slopes):
                part = slope_ref[member : member + 1, :] * unit_ref[member, rows, :].astype(F32)
                cotangent = part if cotangent is None else cotangent + part
            cotangent_half = cotangent.astype(BF16)
            inner = dot(cotangent_half, two_turned[...]) * mid_slope_ref[member, rows, :]
            inner_half = inner.astype(BF16)
            outer = (cotangent + dot(inner_half, one_turned[...])) * gen_slope_ref[member, rows, :]
            sum_two[...] += dot_rows(middle_ref[member, rows, :], cotangent_half)
            sum_one[...] += dot_rows(hidden_ref[member, rows, :], inner_half)
            sum_rows[member] += col_sums(outer)
            total = outer if total is None else total + outer
        new_base[rows, :] = base_ref[rows, :] - base_step * total
        return carry

    lax.fori_loop(0, places // tile, step, 0)
    new_one[...] = one_ref[...] - LEARN_RATE * sum_one[...]
    new_two[...] = two_ref[...] - LEARN_RATE * sum_two[...]
    latent_turned = latent_ref[...].T
    grad_in = jnp.zeros((channels, channels), F32)
    for member in range(batch):
        row = 0.5 * jnp.sum(sum_rows[member], axis=0, keepdims=True)
        grad_in = grad_in + latent_turned[:, member : member + 1] * row
    new_in[...] = in_ref[...] - LEARN_RATE * grad_in
    if which is not None:
        seeds = [seed_ref[which, member] for member in range(batch)]
        gen_forward(seeds, bank_ref, new_in[...], new_base, new_one[...], new_two[...], nexts, tile)


def gen_back(units, slopes, stored, weights, which, seed, bank, tile=256):
    batch, places, channels = units[0].shape
    square = (channels, channels)
    operands = list(units) + list(slopes) + list(stored[1:]) + list(weights)
    outs = [shape(member.shape, F32) for member in weights]
    smem = ()
    if which is not None:
        smem = (len(operands),)
        operands = operands + [seed, bank]
        outs = outs + stored_shapes(batch, places, channels)
    scratch = [
        pltpu.VMEM(square, BF16),
        pltpu.VMEM(square, BF16),
        pltpu.VMEM(square, F32),
        pltpu.VMEM(square, F32),
        pltpu.VMEM((batch, 8, channels), F32),
    ]
    body = functools.partial(gen_back_body, which, tile, len(units), batch)
    results = call(body, outs, scratch, n_inputs=len(operands), smem=smem)(*operands)
    return results[:4], results[4:]


def disc_update_body(batch, reals, is_last, grads_ref, *refs):
    refs = list(refs)
    returns = [refs.pop(0) for _ in range(4)]
    params = [refs.pop(0) for _ in range(3)]
    before = refs.pop(0) if is_last else None
    news = [refs.pop(0) for _ in range(3)]
    last_ref = refs.pop(0)
    channels = params[0].shape[0]
    one = grads_ref[0:channels, :]
    two = grads_ref[channels : 2 * channels, :]
    out = grads_ref[HEAD : HEAD + 1, :]
    verdicts = [grads_ref[HEAD + 1 + i : HEAD + 2 + i, :] for i in range(batch + reals)]
    fakes = verdicts[:batch]
    for back in returns:
        one = one + back[0:channels, :].astype(F32)
        two = two + back[channels : 2 * channels, :].astype(F32)
        tail = back[HEAD:PACKET, :].astype(F32)
        out = out + (tail[0:1, :] + tail[1:2, :])
        for i in range(batch):
            fakes.append(tail[2 + 2 * i : 3 + 2 * i, :] + tail[3 + 2 * i : 4 + 2 * i, :])
    verdicts = fakes + verdicts[batch:]
    updated = [
        member[...] - LEARN_RATE * grad for member, grad in zip(params, (one, two, out))
    ]
    for new, value in zip(news, updated):
        new[...] = value
    lanes = lax.broadcasted_iota(jnp.int32, (1, channels), 1)
    line = jnp.zeros((1, channels), F32)
    for place, value in enumerate(verdicts):
        line = jnp.where(lanes == place, value, line)
    count = len(verdicts)
    if is_last:
        last_ref[0:1, :] = before[0:1, 0:count]
        last_ref[1:2, :] = line[:, 0:count]
    else:
        last_ref[...] = line
        write_packet(refs[0], *updated)


def disc_update(grads, returns, params, before, batch, reals):
    is_last = before is not None
    operands = [grads] + list(returns) + list(params) + ([before] if is_last else [])
    outs = [shape(member.shape, F32) for member in params]
    if is_last:
        outs = outs + [shape((STEPS, 5 * batch + reals), F32)]
    else:
        outs = outs + [shape((1, 128), F32), shape((PACKET, 128), BF16)]
    body = functools.partial(disc_update_body, batch, reals, is_last)
    return call(body, outs, n_inputs=len(operands))(*operands)


def shifted(block, axis, distance):
    count = lax.axis_size(axis)
    return lax.ppermute(block, axis, [(i, (i + distance) % count) for i in range(count)])


SLOTS = (("row", 1), ("row", -1), ("col", 1), ("col", -1))


def on_device(
    data, real_index, latent_seed, latent_bank, g_in, g_base, g_one, g_two, d_one, d_two, d_out
):
    batch = latent_seed.shape[3]
    reals = real_index.shape[3]
    gens = [member[0, 0] for member in (g_in, g_base, g_one, g_two)]
    discs = [d_one[0, 0], d_two[0, 0], d_out[0]]
    seed = latent_seed[0, 0]
    index = real_index[0, 0]
    samples = data[0, 0]
    packet = pack(*discs)
    stored = None
    verdict = None
    for step in range(STEPS):
        is_last = step == STEPS - 1
        arrived = [shifted(packet, axis, -distance) for axis, distance in SLOTS]
        if stored is None:
            stored = generate(seed, step, latent_bank, gens)
        fakes = stored[0]
        own_grads, own_unit, own_slope = judge(packet, fakes, samples, index[step])
        units = [own_unit]
        slopes = [own_slope]
        returns = []
        for (axis, distance), theirs in zip(SLOTS, arrived):
            grads, unit, slope = judge(theirs, fakes)
            returns.append(shifted(grads, axis, distance))
            units.append(unit)
            slopes.append(slope)
        gens, stored = gen_back(
            units, slopes, stored, gens, None if is_last else step + 1, seed, latent_bank
        )
        results = disc_update(
            own_grads, returns, discs, verdict if is_last else None, batch, reals
        )
        discs = results[:3]
        verdict = results[3]
        packet = None if is_last else results[4]
    finals = [member[None, None] for member in gens] + [
        discs[0][None, None],
        discs[1][None, None],
        discs[2][None],
        verdict[None, None],
    ]
    return tuple(finals)


def solution(mesh):
    matrix = P("row", "col", None, None)
    return jax.shard_map(
        on_device,
        mesh=mesh,
        in_specs=(
            P("row", "col", None, None, None),
            matrix,
            matrix,
            P(),
            matrix,
            matrix,
            matrix,
            matrix,
            matrix,
            matrix,
            P("row", "col", None),
        ),
        out_specs=(
            matrix,
            matrix,
            matrix,
            matrix,
            matrix,
            matrix,
            P("row", "col", None),
            matrix,
        ),
        check_vma=False,
    )
```

```python
import functools

import jax
import jax.numpy as jnp
from jax import lax
from jax.experimental import pallas as pl
from jax.experimental.pallas import tpu as pltpu
from jax.sharding import PartitionSpec as P

STEPS = 2
LEARN_RATE = 0.05
BASE_RATE = 0.1
PACKET = 272
HEAD = 256
VMEM_LIMIT = 24 * 1024 * 1024
F32 = jnp.float32
BF16 = jnp.bfloat16


def dot(left, right):
    return jnp.dot(left, right, preferred_element_type=F32)


def dot_rows(left, right):
    return lax.dot_general(left, right, (((0,), (0,)), ((), ())), preferred_element_type=F32)


def silu_parts(half):
    tanh_part = jnp.tanh(half)
    above = 1.0 + tanh_part
    value = half * above
    slope_twice = above + value * (1.0 - tanh_part)
    return value, slope_twice


def sigmoid(value):
    return 0.5 * (1.0 + jnp.tanh(0.5 * value))


def col_sums(tile):
    rows, channels = tile.shape
    return jnp.sum(tile.reshape(rows // 8, 8, channels), axis=0)


def split_two(value):
    high = value.astype(BF16)
    low = (value - high.astype(F32)).astype(BF16)
    return high, low


def shape(dims, dtype):
    return jax.ShapeDtypeStruct(dims, dtype)


def call(body, operands, out_shape, scratch=(), smem=(), hbm=(), flops=0):
    spaces = [pltpu.VMEM] * len(operands)
    for i in range(len(operands)):
        spaces[i] = pltpu.SMEM if i in smem else pltpu.HBM if i in hbm else pltpu.VMEM
    operands = [
        pltpu.with_memory_space_constraint(member, pltpu.HBM) if i in hbm else member
        for i, member in enumerate(operands)
    ]
    return pl.pallas_call(
        body,
        out_shape=tuple(out_shape),
        in_specs=[pl.BlockSpec(memory_space=space) for space in spaces],
        out_specs=tuple(pl.BlockSpec(memory_space=pltpu.VMEM) for _ in out_shape),
        scratch_shapes=list(scratch),
        compiler_params=pltpu.CompilerParams(vmem_limit_bytes=VMEM_LIMIT),
        cost_estimate=pl.CostEstimate(flops=flops, bytes_accessed=flops // 1000, transcendentals=0),
    )(*operands)


def start_all(pairs, semaphores):
    copies = [
        pltpu.make_async_copy(source, target, semaphores.at[i])
        for i, (source, target) in enumerate(pairs)
    ]
    for copy in copies:
        copy.start()
    return copies


def write_packet(packet_ref, one, two, rows):
    channels = one.shape[1]
    packet_ref[0:channels, :] = one.astype(BF16)
    packet_ref[channels:HEAD, :] = two.astype(BF16)
    spot = lax.broadcasted_iota(jnp.int32, (PACKET - HEAD, channels), 0)
    tail = jnp.zeros((PACKET - HEAD, channels), F32)
    for place, row in enumerate(rows):
        high, low = split_two(row)
        tail = jnp.where(spot == 2 * place, high.astype(F32), tail)
        tail = jnp.where(spot == 2 * place + 1, low.astype(F32), tail)
    packet_ref[HEAD:PACKET, :] = tail.astype(BF16)


def packet_row(tail, place):
    return tail[2 * place : 2 * place + 1, :] + tail[2 * place + 1 : 2 * place + 2, :]


def pack_body(one_hbm, two_hbm, out_hbm, packet_ref, one_ref, two_ref, out_ref, semaphores):
    pairs = [(one_hbm, one_ref), (two_hbm, two_ref), (out_hbm, out_ref)]
    for copy in start_all(pairs, semaphores):
        copy.wait()
    write_packet(packet_ref, one_ref[...], two_ref[...], [out_ref[...]])


def pack(params):
    outs = [shape((PACKET, params[0].shape[1]), BF16)] + [shape(m.shape, F32) for m in params]
    results = call(pack_body, params, outs, [pltpu.SemaphoreType.DMA((3,))], hbm=(0, 1, 2))
    return results[0], results[1:]


def dot_turned(left, right):
    return lax.dot_general(left, right, (((1,), (1,)), ((), ())), preferred_element_type=F32)


def unpack(packet_ref):
    channels = packet_ref.shape[1]
    tail = packet_ref[HEAD:PACKET, :].astype(F32)
    return packet_ref[0:channels, :], packet_ref[channels:HEAD, :], tail[0:1, :] + tail[1:2, :]


def both(left, right):
    blank = jnp.zeros_like(left)
    return jnp.concatenate(
        [jnp.concatenate([left, blank], axis=1), jnp.concatenate([blank, right], axis=1)], axis=0
    )


def judge_pair(images, one, two, out_row, shared):
    channels = images.shape[1] if shared else images.shape[1] // 2
    half = BF16(0.5)
    left = slice(0, channels)
    right = slice(channels, 2 * channels)
    one_both = both(*one)
    one_first = jnp.concatenate(one, axis=1) if shared else one_both
    first, slope_first = silu_parts(dot(images, one_first * half))
    first_half = first.astype(BF16)
    two_half = both(*two) * half
    image_half = 0.5 * images.astype(F32)
    if shared:
        image_half = jnp.concatenate([image_half, image_half], axis=1)
    feature, slope_out = silu_parts(image_half + dot(first_half, two_half))
    outer = (0.5 * out_row) * slope_out
    outer_half = outer.astype(BF16)
    inner_half = (dot_turned(outer_half, two_half) * slope_first).astype(BF16)
    unit = outer + dot_turned(inner_half, one_both)
    if shared:
        wide = dot_rows(images, inner_half)
        ones = [wide[:, left], wide[:, right]]
    else:
        ones = [dot_rows(images[:, part], inner_half[:, part]) for part in (left, right)]
    sums = jnp.sum(feature.reshape(-1, 8, 2 * channels), axis=0)
    sums = jnp.sum(sums, axis=0, keepdims=True)
    triples = [
        (ones[i], dot_rows(first_half[:, part], outer_half[:, part]), sums[:, part])
        for i, part in enumerate((left, right))
    ]
    return unit.astype(BF16), triples


def finish(sums, out_row, signs, places, lines_ref):
    count = len(sums)
    channels = out_row.shape[1]
    lines_ref[...] = jnp.zeros_like(lines_ref)
    for member in range(count):
        lines_ref[member : member + 1, :] = sums[member][2]
    features = lines_ref[...]
    scale = 1.0 / places
    verdicts = jnp.sum(features * out_row, axis=1, keepdims=True) * scale
    verdicts = jnp.broadcast_to(verdicts, features.shape)
    spot = lax.broadcasted_iota(jnp.int32, features.shape, 0)
    plus = sigmoid(verdicts) * scale
    minus = -sigmoid(-verdicts) * scale
    slopes = jnp.where(spot < signs, plus, minus)
    total_out = jnp.sum(features * slopes, axis=0, keepdims=True)
    total_one = None
    total_two = None
    for member in range(count):
        slope = slopes[member : member + 1, :]
        part_one = slope * sums[member][0]
        part_two = slope * sums[member][1]
        total_one = part_one if total_one is None else total_one + part_one
        total_two = part_two if total_two is None else total_two + part_two
    return verdicts, minus, total_one, total_two, total_out


def judge_own_body(step, batch, reals, packet_ref, fakes_ref, reals_ref, grads_ref, unit_ref, slope_ref, lines_ref):
    rows, channels = fakes_ref.shape
    places = rows // batch
    one, two, out_row = unpack(packet_ref)
    out_pair = jnp.concatenate([out_row, out_row], axis=1)
    kept = [None] * (batch + reals)
    for member in range(batch):
        span = slice(member * places, (member + 1) * places)
        images = jnp.concatenate([fakes_ref[span, :], reals_ref[step * reals + member]], axis=1)
        unit, triples = judge_pair(images, (one, one), (two, two), out_pair, False)
        unit_ref[span, :] = unit[:, 0:channels]
        kept[member], kept[batch + member] = triples
    verdicts, minus, total_one, total_two, total_out = finish(kept, out_row, batch, places, lines_ref)
    slope_ref[...] = minus
    grads_ref[0:channels, :] = total_one
    grads_ref[channels:HEAD, :] = total_two
    grads_ref[HEAD : HEAD + 8, :] = verdicts
    grads_ref[HEAD + 8 : PACKET, :] = jnp.broadcast_to(total_out, (8, channels))


def judge_own(packet, fakes, reals_rows, step, batch, reals):
    rows, channels = fakes.shape
    outs = [
        shape((PACKET, channels), F32),
        shape((rows, channels), BF16),
        shape((8, channels), F32),
    ]
    body = functools.partial(judge_own_body, step, batch, reals)
    flops = 4 * 6 * 2 * 1024 * 128 * 128
    return call(body, [packet, fakes, reals_rows], outs, [pltpu.VMEM((8, channels), F32)], flops=flops)


def judge_others_body(judges, batch, *refs):
    refs = list(refs)
    packets = [refs.pop(0) for _ in range(judges)]
    fakes_ref = refs.pop(0)
    refs.pop(0)
    grads = [refs.pop(0) for _ in range(judges)]
    units = [refs.pop(0) for _ in range(judges)]
    slope_ref = refs.pop(0)
    lines_ref = refs.pop(0)
    rows, channels = fakes_ref.shape
    places = rows // batch
    kept = [[None] * batch for _ in range(judges)]
    parts = [unpack(packet) for packet in packets]
    for pair in range(0, judges, 2):
        ones, twos, outs = zip(*parts[pair : pair + 2])
        out_pair = jnp.concatenate(outs, axis=1)
        for member in range(batch):
            span = slice(member * places, (member + 1) * places)
            unit, triples = judge_pair(fakes_ref[span, :], ones, twos, out_pair, True)
            for side in range(2):
                units[pair + side][span, :] = unit[:, side * channels : (side + 1) * channels]
                kept[pair + side][member] = triples[side]
    for which in range(judges):
        verdicts, minus, total_one, total_two, total_out = finish(
            kept[which], parts[which][2], batch, places, lines_ref.at[which]
        )
        slope_ref[which * batch : (which + 1) * batch, :] = minus[0:batch, :]
        tail = [total_out] + [verdicts[member : member + 1, :] for member in range(batch)]
        write_packet(grads[which], total_one, total_two, tail)


def judge_others(packets, fakes, batch, after):
    rows, channels = fakes.shape
    judges = len(packets)
    outs = [shape((PACKET, channels), BF16)] * judges
    outs = outs + [shape((rows, channels), BF16)] * judges
    outs = outs + [shape((judges * batch, channels), F32)]
    body = functools.partial(judge_others_body, judges, batch)
    scratch = [pltpu.VMEM((judges, 8, channels), F32)]
    flops = 8 * 6 * 2 * 1024 * 128 * 128
    results = call(body, list(packets) + [fakes, after], outs, scratch, flops=flops)
    return results[:judges], results[judges : 2 * judges], results[2 * judges]


def twice(tile):
    return jnp.concatenate([tile, tile], axis=1)


def gen_forward(latent, w_in, base, w_one, w_two, outs):
    fakes_ref, hidden_ref, middle_ref, gen_slope_ref, mid_slope_ref = outs
    places, channels = base.shape
    shifted = 0.5 * dot(latent.astype(BF16), w_in.astype(BF16))
    shift_row = jnp.concatenate([shifted[0:1, :], shifted[1:2, :]], axis=1)
    one = w_one.astype(BF16) * BF16(0.5)
    two = w_two.astype(BF16)
    hidden, slope_gen = silu_parts(twice(0.5 * base.astype(BF16).astype(F32)) + shift_row)
    hidden_half = hidden.astype(BF16)
    middle, slope_mid = silu_parts(dot(hidden_half, both(one, one)))
    middle_half = middle.astype(BF16)
    fakes = (hidden_half.astype(F32) + dot(middle_half, both(two, two))).astype(BF16)
    fakes_ref[0:places, :] = fakes[:, 0:channels]
    fakes_ref[places : 2 * places, :] = fakes[:, channels : 2 * channels]
    hidden_ref[...] = hidden_half
    middle_ref[...] = middle_half
    gen_slope_ref[...] = slope_gen
    mid_slope_ref[...] = slope_mid


def stored_shapes(places, channels):
    wide = (places, 2 * channels)
    return [
        shape((2 * places, channels), BF16),
        shape(wide, BF16),
        shape(wide, BF16),
        shape(wide, F32),
        shape(wide, F32),
    ]


def begin_body(batch, reals, seed_hbm, index_hbm, *refs):
    bank, data, *weights = refs[:6]
    weight_refs = refs[6:10]
    latent_ref, reals_ref = refs[10:12]
    outs = refs[12:17]
    raw_ref, seed_ref, index_ref, semaphores = refs[17:]
    count = len(weights)
    copies = start_all(list(zip(weights, weight_refs)), semaphores)
    chosen = start_all(
        [(seed_hbm, seed_ref), (index_hbm, index_ref)], semaphores.at[pl.ds(count, 2)]
    )
    raw_ref[...] = jnp.zeros_like(raw_ref)
    for copy in chosen:
        copy.wait()
    early = []
    late = []
    for step in range(STEPS):
        for member in range(batch):
            early.append(
                (bank.at[pl.ds(seed_ref[step, member], 1)], raw_ref.at[step, pl.ds(member, 1)])
            )
        for member in range(reals):
            late.append((data.at[index_ref[step, member]], reals_ref.at[step * reals + member]))
    rest = len(early + late)
    others = start_all(early + late, semaphores.at[pl.ds(count + 2, rest)])
    copies = copies + others
    for copy in copies[: count + len(early)]:
        copy.wait()
    latent_ref[...] = raw_ref[...].astype(BF16).astype(F32)
    w_in, base, w_one, w_two = [ref[...] for ref in weight_refs]
    gen_forward(latent_ref[0], w_in, base, w_one, w_two, outs)
    for copy in copies[count + len(early) :]:
        copy.wait()


def begin(seed, index, bank, data, weights):
    batch = seed.shape[1]
    reals = index.shape[1]
    places, channels = weights[1].shape
    outs = [shape(member.shape, F32) for member in weights]
    outs = outs + [shape((STEPS, 8, channels), F32), shape((STEPS * reals, places, channels), BF16)]
    outs = outs + stored_shapes(places, channels)
    scratch = [
        pltpu.VMEM((STEPS, 8, channels), F32),
        pltpu.SMEM(seed.shape, jnp.int32),
        pltpu.SMEM(index.shape, jnp.int32),
        pltpu.SemaphoreType.DMA((len(weights) + 2 + STEPS * (batch + reals),)),
    ]
    operands = [seed, index, bank, data] + list(weights)
    body = functools.partial(begin_body, batch, reals)
    flops = 4 * 2 * 1024 * 128 * 128
    results = call(body, operands, outs, scratch, hbm=range(8), flops=flops)
    return results[:4], results[4], results[5], results[6:]


def gen_back_body(step, judges, *refs):
    is_last = step == STEPS - 1
    refs = list(refs)
    units = [refs.pop(0) for _ in range(judges)]
    own_slope, other_slopes = [refs.pop(0) for _ in range(2)]
    hidden_ref, middle_ref, gen_slope_ref, mid_slope_ref, latent_ref = [refs.pop(0) for _ in range(5)]
    in_ref, base_ref, one_ref, two_ref = [refs.pop(0) for _ in range(4)]
    new_in, new_base, new_one, new_two = [refs.pop(0) for _ in range(4)]
    places, channels = base_ref.shape
    sides = (slice(0, channels), slice(channels, 2 * channels))
    spans = (slice(0, places), slice(places, 2 * places))

    halves = []
    for member, span in enumerate(spans):
        total = own_slope[member : member + 1, :] * units[0][span, :].astype(F32)
        for which in range(1, judges):
            place = 2 * (which - 1) + member
            total = total + other_slopes[place : place + 1, :] * units[which][span, :].astype(F32)
        halves.append(total)
    cotangent = jnp.concatenate(halves, axis=1)
    cotangent_half = cotangent.astype(BF16)
    one = one_ref[...].astype(BF16)
    two = two_ref[...].astype(BF16) * BF16(0.5)
    inner_half = (dot_turned(cotangent_half, both(two, two)) * mid_slope_ref[...]).astype(BF16)
    outer = (cotangent + dot_turned(inner_half, both(one, one))) * gen_slope_ref[...]
    grad_two = [dot_rows(middle_ref[:, side], cotangent_half[:, side]) for side in sides]
    grad_one = [dot_rows(hidden_ref[:, side], inner_half[:, side]) for side in sides]
    sums = jnp.sum(jnp.sum(outer.reshape(-1, 8, 2 * channels), axis=0), axis=0, keepdims=True)
    latent_turned = latent_ref[step].T
    grad_in = [
        latent_turned[:, member : member + 1] * (0.5 * sums[:, side])
        for member, side in enumerate(sides)
    ]
    base = base_ref[...] - (0.5 * BASE_RATE * places) * (outer[:, sides[0]] + outer[:, sides[1]])
    w_one = one_ref[...] - LEARN_RATE * (grad_one[0] + grad_one[1])
    w_two = two_ref[...] - LEARN_RATE * (grad_two[0] + grad_two[1])
    w_in = in_ref[...] - LEARN_RATE * (grad_in[0] + grad_in[1])
    new_in[...] = w_in
    new_base[...] = base
    new_one[...] = w_one
    new_two[...] = w_two
    if not is_last:
        gen_forward(latent_ref[step + 1], w_in, base, w_one, w_two, refs)


def gen_back(step, units, own_slope, other_slopes, stored, latents, weights):
    places, channels = weights[1].shape
    operands = list(units) + [own_slope, other_slopes] + list(stored[1:]) + [latents] + list(weights)
    outs = [shape(member.shape, F32) for member in weights]
    if step < STEPS - 1:
        outs = outs + stored_shapes(places, channels)
    body = functools.partial(gen_back_body, step, len(units))
    flops = 12 * 2 * 1024 * 128 * 128
    results = call(body, operands, outs, flops=flops)
    return results[:4], results[4:]


def disc_update_body(batch, reals, is_last, grads_ref, *refs):
    refs = list(refs)
    returns = [refs.pop(0) for _ in range(4)]
    refs.pop(0)
    params = [refs.pop(0) for _ in range(3)]
    before = refs.pop(0) if is_last else None
    news = [refs.pop(0) for _ in range(3)]
    last_ref = refs.pop(0)
    channels = params[0].shape[0]
    one = grads_ref[0:channels, :]
    two = grads_ref[channels:HEAD, :]
    out = grads_ref[HEAD + 8 : HEAD + 9, :]
    verdicts = [grads_ref[HEAD + i : HEAD + 1 + i, :] for i in range(batch + reals)]
    tails = []
    for back in returns:
        one = one + back[0:channels, :].astype(F32)
        two = two + back[channels:HEAD, :].astype(F32)
        tail = back[HEAD:PACKET, :].astype(F32)
        out = out + packet_row(tail, 0)
        tails.append([packet_row(tail, 1 + i) for i in range(batch)])
    ordered = verdicts[:batch]
    for axis, (inner, outer) in (("row", tails[0:2]), ("col", tails[2:4])):
        is_odd = lax.rem(lax.axis_index(axis), 2) == 1
        ordered = ordered + [jnp.where(is_odd, a, b) for a, b in zip(inner, outer)]
        ordered = ordered + [jnp.where(is_odd, b, a) for a, b in zip(inner, outer)]
    ordered = ordered + verdicts[batch:]
    updated = [member[...] - LEARN_RATE * grad for member, grad in zip(params, (one, two, out))]
    for new, value in zip(news, updated):
        new[...] = value
    lanes = lax.broadcasted_iota(jnp.int32, (1, channels), 1)
    line = jnp.zeros((1, channels), F32)
    for place, value in enumerate(ordered):
        line = jnp.where(lanes == place, value, line)
    count = len(ordered)
    if is_last:
        last_ref[0:1, :] = before[0:1, 0:count]
        last_ref[1:2, :] = line[:, 0:count]
    else:
        last_ref[...] = line
        write_packet(refs[0], updated[0], updated[1], [updated[2]])


def disc_update(grads, returns, after, params, before, batch, reals):
    is_last = before is not None
    operands = [grads] + list(returns) + [after] + list(params) + ([before] if is_last else [])
    outs = [shape(member.shape, F32) for member in params]
    if is_last:
        outs = outs + [shape((STEPS, 5 * batch + reals), F32)]
    else:
        outs = outs + [shape((1, 128), F32), shape((PACKET, 128), BF16)]
    body = functools.partial(disc_update_body, batch, reals, is_last)
    return call(body, operands, outs, hbm=(5,) if is_last else ())


def paired(block, axis, offset):
    count = lax.axis_size(axis)
    route = []
    for i in range(0, count, 2):
        first, second = (i + offset) % count, (i + offset + 1) % count
        route += [(first, second), (second, first)]
    return lax.ppermute(block, axis, route)


EDGES = (("row", 0), ("row", 1), ("col", 0), ("col", 1))


def on_device(
    data, real_index, latent_seed, latent_bank, g_in, g_base, g_one, g_two, d_one, d_two, d_out
):
    batch = latent_seed.shape[3]
    reals = real_index.shape[3]
    packet, discs = pack([d_one[0, 0], d_two[0, 0], d_out[0]])
    verdict = None
    for step in range(STEPS):
        is_last = step == STEPS - 1
        arrived = [paired(packet, axis, offset) for axis, offset in EDGES]
        if step == 0:
            gens, latents, reals_rows, stored = begin(
                latent_seed[0, 0],
                real_index[0, 0],
                latent_bank,
                data[0, 0],
                [member[0, 0] for member in (g_in, g_base, g_one, g_two)],
            )
        fakes = stored[0]
        own_grads, own_unit, own_slope = judge_own(packet, fakes, reals_rows, step, batch, reals)
        grads, units, other_slopes = judge_others(arrived, fakes, batch, own_slope)
        returns = [paired(member, axis, offset) for member, (axis, offset) in zip(grads, EDGES)]
        gens, stored = gen_back(
            step, [own_unit] + list(units), own_slope, other_slopes, stored, latents, gens
        )
        results = disc_update(
            own_grads, returns, gens[0], discs, verdict if is_last else None, batch, reals
        )
        discs = results[:3]
        verdict = results[3]
        packet = None if is_last else results[4]
    finals = [member[None, None] for member in gens] + [
        discs[0][None, None],
        discs[1][None, None],
        discs[2][None],
        verdict[None, None],
    ]
    return tuple(finals)


def solution(mesh):
    matrix = P("row", "col", None, None)
    return jax.shard_map(
        on_device,
        mesh=mesh,
        in_specs=(
            P("row", "col", None, None, None),
            matrix,
            matrix,
            P(),
            matrix,
            matrix,
            matrix,
            matrix,
            matrix,
            matrix,
            P("row", "col", None),
        ),
        out_specs=(
            matrix,
            matrix,
            matrix,
            matrix,
            matrix,
            matrix,
            P("row", "col", None),
            matrix,
        ),
        check_vma=False,
    )
```

```python
import functools

import jax
import jax.numpy as jnp
from jax import lax
from jax.experimental import pallas as pl
from jax.experimental.pallas import tpu as pltpu
from jax.sharding import PartitionSpec as P

STEPS = 2
LEARN_RATE = 0.05
BASE_RATE = 0.1
PACKET = 272
HEAD = 256
VMEM_LIMIT = 24 * 1024 * 1024
F32 = jnp.float32
BF16 = jnp.bfloat16


def dot(left, right):
    return jnp.dot(left, right, preferred_element_type=F32)


def dot_rows(left, right):
    return lax.dot_general(left, right, (((0,), (0,)), ((), ())), preferred_element_type=F32)


def silu_parts(half):
    above = 1.0 + jnp.tanh(half)
    value = half * above
    value_half = value.astype(BF16)
    above_half = above.astype(BF16)
    return value, value_half, above_half + value_half * (BF16(2.0) - above_half)


def silu_exact(half):
    above = 1.0 + jnp.tanh(half)
    value = half * above
    return value, above + value * (2.0 - above)


def sigmoid(value):
    return 0.5 * (1.0 + jnp.tanh(0.5 * value))


def split_two(value):
    high = value.astype(BF16)
    low = (value - high.astype(F32)).astype(BF16)
    return high, low


def shape(dims, dtype):
    return jax.ShapeDtypeStruct(dims, dtype)


def call(body, operands, out_shape, scratch=(), smem=(), hbm=(), flops=0):
    spaces = [pltpu.VMEM] * len(operands)
    for i in range(len(operands)):
        spaces[i] = pltpu.SMEM if i in smem else pltpu.HBM if i in hbm else pltpu.VMEM
    operands = [
        pltpu.with_memory_space_constraint(member, pltpu.HBM) if i in hbm else member
        for i, member in enumerate(operands)
    ]
    return pl.pallas_call(
        body,
        out_shape=tuple(out_shape),
        in_specs=[pl.BlockSpec(memory_space=space) for space in spaces],
        out_specs=tuple(pl.BlockSpec(memory_space=pltpu.VMEM) for _ in out_shape),
        scratch_shapes=list(scratch),
        compiler_params=pltpu.CompilerParams(vmem_limit_bytes=VMEM_LIMIT),
        cost_estimate=pl.CostEstimate(flops=flops, bytes_accessed=flops // 1000, transcendentals=0),
    )(*operands)


def start_all(pairs, semaphores):
    copies = [
        pltpu.make_async_copy(source, target, semaphores.at[i])
        for i, (source, target) in enumerate(pairs)
    ]
    for copy in copies:
        copy.start()
    return copies


def write_packet(packet_ref, one, two, rows):
    channels = one.shape[1]
    packet_ref[0:channels, :] = one.astype(BF16)
    packet_ref[channels:HEAD, :] = two.astype(BF16)
    spot = lax.broadcasted_iota(jnp.int32, (PACKET - HEAD, channels), 0)
    tail = jnp.zeros((PACKET - HEAD, channels), F32)
    for place, row in enumerate(rows):
        high, low = split_two(row)
        tail = jnp.where(spot == 2 * place, high.astype(F32), tail)
        tail = jnp.where(spot == 2 * place + 1, low.astype(F32), tail)
    packet_ref[HEAD:PACKET, :] = tail.astype(BF16)


def packet_row(tail, place):
    return tail[2 * place : 2 * place + 1, :] + tail[2 * place + 1 : 2 * place + 2, :]


def pack_body(one_hbm, two_hbm, out_hbm, packet_ref, one_ref, two_ref, out_ref, semaphores):
    pairs = [(one_hbm, one_ref), (two_hbm, two_ref), (out_hbm, out_ref)]
    for copy in start_all(pairs, semaphores):
        copy.wait()
    write_packet(packet_ref, one_ref[...], two_ref[...], [out_ref[...]])


def pack(params):
    outs = [shape((PACKET, params[0].shape[1]), BF16)] + [shape(m.shape, F32) for m in params]
    results = call(pack_body, params, outs, [pltpu.SemaphoreType.DMA((3,))], hbm=(0, 1, 2))
    return results[0], results[1:]


def dot_turned(left, right):
    return lax.dot_general(left, right, (((1,), (1,)), ((), ())), preferred_element_type=F32)


def unpack(packet_ref):
    channels = packet_ref.shape[1]
    tail = packet_ref[HEAD:PACKET, :].astype(F32)
    return packet_ref[0:channels, :], packet_ref[channels:HEAD, :], tail[0:1, :] + tail[1:2, :]


def both(left, right):
    blank = jnp.zeros_like(left)
    return jnp.concatenate(
        [jnp.concatenate([left, blank], axis=1), jnp.concatenate([blank, right], axis=1)], axis=0
    )


OFFSET = 2


def judge_steps(pair, result):
    images, one, two, out_row, shared = pair
    half = BF16(0.5)
    one_first = jnp.concatenate(one, axis=1) if shared else both(*one)
    halves = dot(images, one_first * half)
    yield
    _, first_half, slope_first = silu_parts(halves)
    image_half = 0.5 * images.astype(F32)
    if shared:
        image_half = twice(image_half)
    product = dot(first_half, both(*two) * half)
    yield
    feature, slope_out = silu_exact(image_half + product)
    sums = jnp.sum(feature.reshape(-1, 8, feature.shape[1]), axis=0)
    sums = jnp.sum(sums, axis=0, keepdims=True)
    outer = (0.5 * out_row) * slope_out
    outer_half = outer.astype(BF16)
    product = dot_turned(outer_half, both(*two) * half)
    yield
    inner_half = product.astype(BF16) * slope_first
    product = dot_turned(inner_half, both(*one))
    channels = inner_half.shape[1] // 2
    sides = [slice(0, channels), slice(channels, 2 * channels)]
    grad_two = [dot_rows(first_half[:, s], outer_half[:, s]) for s in sides]
    yield
    result.append((outer + product).astype(BF16))
    if shared:
        wide = dot_rows(images, inner_half)
        grad_one = [wide[:, s] for s in sides]
    else:
        grad_one = [dot_rows(images[:, s], inner_half[:, s]) for s in sides]
    for i, s in enumerate(sides):
        result.append((grad_one[i], grad_two[i], sums[:, s]))


def judge_pairs(pairs):
    results = [[] for _ in pairs]
    works = [judge_steps(pair, result) for pair, result in zip(pairs, results)]
    beat = 0
    left = set(range(len(works)))
    while left:
        for place in sorted(left):
            if beat >= place * OFFSET and next(works[place], True):
                left.discard(place)
        beat += 1
    return results


def verdict_lines(triples, out_rows, signs, places, lines_ref):
    lines_ref[...] = jnp.zeros_like(lines_ref)
    spot = lax.broadcasted_iota(jnp.int32, lines_ref.shape, 0)
    outs = jnp.zeros(lines_ref.shape, F32)
    is_fake = jnp.zeros(lines_ref.shape, jnp.bool_)
    for member, (triple, out_row) in enumerate(zip(triples, out_rows)):
        lines_ref[member : member + 1, :] = triple[2]
        outs = jnp.where(spot == member, out_row, outs)
        if signs[member]:
            is_fake = is_fake | (spot == member)
    features = lines_ref[...]
    scale = 1.0 / places
    verdicts = jnp.sum(features * outs, axis=1, keepdims=True) * scale
    verdicts = jnp.broadcast_to(verdicts, features.shape)
    plus = sigmoid(verdicts) * scale
    minus = -sigmoid(-verdicts) * scale
    return verdicts, minus, jnp.where(is_fake, plus, minus)


def weigh(triples, slopes):
    totals = None
    for triple, slope in zip(triples, slopes):
        parts = [slope * member for member in triple]
        totals = parts if totals is None else [x + y for x, y in zip(totals, parts)]
    return totals


def judge_own_body(step, batch, reals, packet_ref, fakes_ref, reals_ref, _, grads_ref, unit_ref, slope_ref, lines_ref):
    rows, channels = fakes_ref.shape
    places = rows // batch
    one, two, out_row = unpack(packet_ref)
    out_pair = twice(out_row)
    pairs = []
    for member in range(batch):
        span = slice(member * places, (member + 1) * places)
        images = jnp.concatenate([fakes_ref[span, :], reals_ref[step * reals + member]], axis=1)
        pairs.append((images, (one, one), (two, two), out_pair, False))
    results = judge_pairs(pairs)
    for member, result in enumerate(results):
        unit_ref[member * places : (member + 1) * places, :] = result[0][:, 0:channels]
    triples = [result[1] for result in results] + [result[2] for result in results]
    signs = [1] * batch + [0] * reals
    verdicts, minus, slopes = verdict_lines(triples, [out_row] * len(signs), signs, places, lines_ref)
    total_one, total_two, total_out = weigh(triples, [slopes[i : i + 1, :] for i in range(len(signs))])
    slope_ref[...] = minus
    grads_ref[0:channels, :] = total_one
    grads_ref[channels:HEAD, :] = total_two
    grads_ref[HEAD : HEAD + 8, :] = verdicts
    grads_ref[HEAD + 8 : PACKET, :] = jnp.broadcast_to(total_out, (8, channels))


def judge_own(packet, fakes, reals_rows, after, step, batch, reals):
    rows, channels = fakes.shape
    outs = [
        shape((PACKET, channels), F32),
        shape((rows, channels), BF16),
        shape((8, channels), F32),
    ]
    body = functools.partial(judge_own_body, step, batch, reals)
    flops = 4 * 6 * 2 * 1024 * 128 * 128
    return call(body, [packet, fakes, reals_rows, after], outs, [pltpu.VMEM((8, channels), F32)], flops=flops)


def judge_others_body(judges, batch, *refs):
    refs = list(refs)
    packets = [refs.pop(0) for _ in range(judges)]
    fakes_ref = refs.pop(0)
    refs.pop(0)
    grads = [refs.pop(0) for _ in range(judges)]
    units = [refs.pop(0) for _ in range(judges)]
    slope_ref = refs.pop(0)
    lines_ref = refs.pop(0)
    rows, channels = fakes_ref.shape
    places = rows // batch
    parts = [unpack(packet) for packet in packets]
    spans = [slice(member * places, (member + 1) * places) for member in range(batch)]
    pairs = []
    homes = []
    for which in range(0, judges - 1, 2):
        ones, twos, outs = zip(*parts[which : which + 2])
        for member, span in enumerate(spans):
            pairs.append((fakes_ref[span, :], ones, twos, jnp.concatenate(outs, axis=1), True))
            homes.append(((which, member), (which + 1, member)))
    if judges % 2:
        one, two, out_row = parts[-1]
        images = jnp.concatenate([fakes_ref[span, :] for span in spans], axis=1)
        pairs.append((images, (one, one), (two, two), twice(out_row), False))
        homes.append(tuple((judges - 1, member) for member in range(batch)))
    found = {}
    for result, home in zip(judge_pairs(pairs), homes):
        for side, (which, member) in enumerate(home):
            units[which][spans[member], :] = result[0][:, side * channels : (side + 1) * channels]
            found[which, member] = result[1 + side]
    keys = sorted(found)
    triples = [found[key] for key in keys]
    out_rows = [parts[which][2] for which, _ in keys]
    verdicts, minus, slopes = verdict_lines(triples, out_rows, [1] * len(triples), places, lines_ref)
    slope_ref[...] = minus
    for which in range(judges):
        mine = range(which * batch, (which + 1) * batch)
        totals = weigh([triples[i] for i in mine], [slopes[i : i + 1, :] for i in mine])
        tail = [totals[2]] + [verdicts[i : i + 1, :] for i in mine]
        write_packet(grads[which], totals[0], totals[1], tail)


def judge_others(packets, fakes, batch, after):
    rows, channels = fakes.shape
    judges = len(packets)
    outs = [shape((PACKET, channels), BF16)] * judges
    outs = outs + [shape((rows, channels), BF16)] * judges
    outs = outs + [shape((8, channels), F32)]
    body = functools.partial(judge_others_body, judges, batch)
    scratch = [pltpu.VMEM((8, channels), F32)]
    flops = 8 * 6 * 2 * 1024 * 128 * 128
    results = call(body, list(packets) + [fakes, after], outs, scratch, flops=flops)
    return results[:judges], results[judges : 2 * judges], results[2 * judges]


def twice(tile):
    return jnp.concatenate([tile, tile], axis=1)


def gen_forward(latent, w_in, base, w_one, w_two, outs):
    fakes_ref, hidden_ref, middle_ref, gen_slope_ref, mid_slope_ref = outs
    places, channels = base.shape
    shifted = 0.5 * dot(latent.astype(BF16), w_in.astype(BF16))
    shift_row = jnp.concatenate([shifted[0:1, :], shifted[1:2, :]], axis=1)
    one = w_one.astype(BF16) * BF16(0.5)
    two = w_two.astype(BF16)
    _, hidden_half, slope_gen = silu_parts(twice(0.5 * base.astype(BF16).astype(F32)) + shift_row)
    _, middle_half, slope_mid = silu_parts(dot(hidden_half, both(one, one)))
    fakes = (hidden_half.astype(F32) + dot(middle_half, both(two, two))).astype(BF16)
    fakes_ref[0:places, :] = fakes[:, 0:channels]
    fakes_ref[places : 2 * places, :] = fakes[:, channels : 2 * channels]
    hidden_ref[...] = hidden_half
    middle_ref[...] = middle_half
    gen_slope_ref[...] = slope_gen
    mid_slope_ref[...] = slope_mid


def stored_shapes(places, channels):
    wide = (places, 2 * channels)
    return [
        shape((2 * places, channels), BF16),
        shape(wide, BF16),
        shape(wide, BF16),
        shape(wide, BF16),
        shape(wide, BF16),
    ]


def begin_body(batch, reals, seed_hbm, index_hbm, *refs):
    bank, data, *weights = refs[:6]
    weight_refs = refs[6:10]
    latent_ref, reals_ref = refs[10:12]
    outs = refs[12:17]
    raw_ref, seed_ref, index_ref, semaphores = refs[17:]
    count = len(weights)
    copies = start_all(list(zip(weights, weight_refs)), semaphores)
    chosen = start_all(
        [(seed_hbm, seed_ref), (index_hbm, index_ref)], semaphores.at[pl.ds(count, 2)]
    )
    raw_ref[...] = jnp.zeros_like(raw_ref)
    for copy in chosen:
        copy.wait()
    early = []
    late = []
    for step in range(STEPS):
        for member in range(batch):
            early.append(
                (bank.at[pl.ds(seed_ref[step, member], 1)], raw_ref.at[step, pl.ds(member, 1)])
            )
        for member in range(reals):
            late.append((data.at[index_ref[step, member]], reals_ref.at[step * reals + member]))
    rest = len(early + late)
    others = start_all(early + late, semaphores.at[pl.ds(count + 2, rest)])
    copies = copies + others
    for copy in copies[: count + len(early)]:
        copy.wait()
    latent_ref[...] = raw_ref[...].astype(BF16).astype(F32)
    w_in, base, w_one, w_two = [ref[...] for ref in weight_refs]
    gen_forward(latent_ref[0], w_in, base, w_one, w_two, outs)
    for copy in copies[count + len(early) :]:
        copy.wait()


def begin(seed, index, bank, data, weights):
    batch = seed.shape[1]
    reals = index.shape[1]
    places, channels = weights[1].shape
    outs = [shape(member.shape, F32) for member in weights]
    outs = outs + [shape((STEPS, 8, channels), F32), shape((STEPS * reals, places, channels), BF16)]
    outs = outs + stored_shapes(places, channels)
    scratch = [
        pltpu.VMEM((STEPS, 8, channels), F32),
        pltpu.SMEM(seed.shape, jnp.int32),
        pltpu.SMEM(index.shape, jnp.int32),
        pltpu.SemaphoreType.DMA((len(weights) + 2 + STEPS * (batch + reals),)),
    ]
    operands = [seed, index, bank, data] + list(weights)
    body = functools.partial(begin_body, batch, reals)
    flops = 4 * 2 * 1024 * 128 * 128
    results = call(body, operands, outs, scratch, hbm=range(8), flops=flops)
    return results[:4], results[4], results[5], results[6:]


def gen_back_body(step, judges, groups, *refs):
    is_last = step == STEPS - 1
    refs = list(refs)
    units = [refs.pop(0) for _ in range(judges)]
    slopes = [refs.pop(0) for _ in range(1 + len(groups))]
    hidden_ref, middle_ref, gen_slope_ref, mid_slope_ref, latent_ref = [refs.pop(0) for _ in range(5)]
    in_ref, base_ref, one_ref, two_ref = [refs.pop(0) for _ in range(4)]
    new_in, new_base, new_one, new_two = [refs.pop(0) for _ in range(4)]
    places, channels = base_ref.shape
    sides = (slice(0, channels), slice(channels, 2 * channels))
    spans = (slice(0, places), slice(places, 2 * places))

    halves = []
    for member, span in enumerate(spans):
        total = slopes[0][member : member + 1, :] * units[0][span, :].astype(F32)
        others = iter(units[1:])
        for slope_ref, size in zip(slopes[1:], groups):
            for which in range(size):
                place = which * len(spans) + member
                unit_ref = next(others)
                total = total + slope_ref[place : place + 1, :] * unit_ref[span, :].astype(F32)
        halves.append(total)
    cotangent = jnp.concatenate(halves, axis=1)
    cotangent_half = cotangent.astype(BF16)
    one = one_ref[...].astype(BF16)
    two = two_ref[...].astype(BF16) * BF16(0.5)
    inner_half = (dot_turned(cotangent_half, both(two, two)).astype(BF16) * mid_slope_ref[...])
    outer = (cotangent + dot_turned(inner_half, both(one, one))) * gen_slope_ref[...].astype(F32)
    grad_two = [dot_rows(middle_ref[:, side], cotangent_half[:, side]) for side in sides]
    grad_one = [dot_rows(hidden_ref[:, side], inner_half[:, side]) for side in sides]
    sums = jnp.sum(jnp.sum(outer.reshape(-1, 8, 2 * channels), axis=0), axis=0, keepdims=True)
    latent_turned = latent_ref[step].T
    grad_in = [
        latent_turned[:, member : member + 1] * (0.5 * sums[:, side])
        for member, side in enumerate(sides)
    ]
    base = base_ref[...] - (0.5 * BASE_RATE * places) * (outer[:, sides[0]] + outer[:, sides[1]])
    w_one = one_ref[...] - LEARN_RATE * (grad_one[0] + grad_one[1])
    w_two = two_ref[...] - LEARN_RATE * (grad_two[0] + grad_two[1])
    w_in = in_ref[...] - LEARN_RATE * (grad_in[0] + grad_in[1])
    new_in[...] = w_in
    new_base[...] = base
    new_one[...] = w_one
    new_two[...] = w_two
    if not is_last:
        gen_forward(latent_ref[step + 1], w_in, base, w_one, w_two, refs)


def gen_back(step, units, slopes, groups, stored, latents, weights):
    places, channels = weights[1].shape
    operands = list(units) + list(slopes) + list(stored[1:]) + [latents] + list(weights)
    outs = [shape(member.shape, F32) for member in weights]
    if step < STEPS - 1:
        outs = outs + stored_shapes(places, channels)
    body = functools.partial(gen_back_body, step, len(units), groups)
    flops = 12 * 2 * 1024 * 128 * 128
    results = call(body, operands, outs, flops=flops)
    return results[:4], results[4:]


def disc_update_body(batch, reals, is_last, grads_ref, *refs):
    refs = list(refs)
    returns = [refs.pop(0) for _ in range(4)]
    refs.pop(0)
    params = [refs.pop(0) for _ in range(3)]
    before = refs.pop(0) if is_last else None
    news = [refs.pop(0) for _ in range(3)]
    last_ref = refs.pop(0)
    channels = params[0].shape[0]
    one = grads_ref[0:channels, :]
    two = grads_ref[channels:HEAD, :]
    out = grads_ref[HEAD + 8 : HEAD + 9, :]
    verdicts = [grads_ref[HEAD + i : HEAD + 1 + i, :] for i in range(batch + reals)]
    tails = []
    for back in returns:
        one = one + back[0:channels, :].astype(F32)
        two = two + back[channels:HEAD, :].astype(F32)
        tail = back[HEAD:PACKET, :].astype(F32)
        out = out + packet_row(tail, 0)
        tails.append([packet_row(tail, 1 + i) for i in range(batch)])
    ordered = verdicts[:batch]
    for axis, (inner, outer) in (("row", (tails[2], tails[1])), ("col", (tails[3], tails[0]))):
        is_odd = lax.rem(lax.axis_index(axis), 2) == 1
        ordered = ordered + [jnp.where(is_odd, a, b) for a, b in zip(inner, outer)]
        ordered = ordered + [jnp.where(is_odd, b, a) for a, b in zip(inner, outer)]
    ordered = ordered + verdicts[batch:]
    updated = [member[...] - LEARN_RATE * grad for member, grad in zip(params, (one, two, out))]
    for new, value in zip(news, updated):
        new[...] = value
    lanes = lax.broadcasted_iota(jnp.int32, (1, channels), 1)
    line = jnp.zeros((1, channels), F32)
    for place, value in enumerate(ordered):
        line = jnp.where(lanes == place, value, line)
    count = len(ordered)
    if is_last:
        last_ref[0:1, :] = before[0:1, 0:count]
        last_ref[1:2, :] = line[:, 0:count]
    else:
        last_ref[...] = line
        write_packet(refs[0], updated[0], updated[1], [updated[2]])


def disc_update(grads, returns, after, params, before, batch, reals):
    is_last = before is not None
    operands = [grads] + list(returns) + [after] + list(params) + ([before] if is_last else [])
    outs = [shape(member.shape, F32) for member in params]
    if is_last:
        outs = outs + [shape((STEPS, 5 * batch + reals), F32)]
    else:
        outs = outs + [shape((1, 128), F32), shape((PACKET, 128), BF16)]
    body = functools.partial(disc_update_body, batch, reals, is_last)
    return call(body, operands, outs, hbm=(5,) if is_last else ())


def paired(block, axis, offset):
    count = lax.axis_size(axis)
    route = []
    for i in range(0, count, 2):
        first, second = (i + offset) % count, (i + offset + 1) % count
        route += [(first, second), (second, first)]
    return lax.ppermute(block, axis, route)


EDGES = (("col", 1), ("row", 1), ("row", 0), ("col", 0))
GROUPS = ((0, 1, 2, 3),)


def on_device(
    data, real_index, latent_seed, latent_bank, g_in, g_base, g_one, g_two, d_one, d_two, d_out
):
    batch = latent_seed.shape[3]
    reals = real_index.shape[3]
    packet, discs = pack([d_one[0, 0], d_two[0, 0], d_out[0]])
    verdict = None
    for step in range(STEPS):
        is_last = step == STEPS - 1
        arrived = [paired(packet, axis, offset) for axis, offset in EDGES]
        if step == 0:
            gens, latents, reals_rows, stored = begin(
                latent_seed[0, 0],
                real_index[0, 0],
                latent_bank,
                data[0, 0],
                [member[0, 0] for member in (g_in, g_base, g_one, g_two)],
            )
        fakes = stored[0]
        returns = [None] * len(EDGES)
        units = [None] * len(EDGES)
        own_grads, own_unit, after = judge_own(packet, fakes, reals_rows, stored[1], step, batch, reals)
        slopes = [after]
        for group in GROUPS:
            grads, some, after = judge_others([arrived[i] for i in group], fakes, batch, after)
            slopes.append(after)
            for i, grad, unit in zip(group, grads, some):
                returns[i] = paired(grad, *EDGES[i])
                units[i] = unit
        units = [own_unit] + [units[i] for group in GROUPS for i in group]
        sizes = [len(group) for group in GROUPS]
        gens, stored = gen_back(step, units, slopes, sizes, stored, latents, gens)
        results = disc_update(
            own_grads, returns, gens[0], discs, verdict if is_last else None, batch, reals
        )
        discs = results[:3]
        verdict = results[3]
        packet = None if is_last else results[4]
    finals = [member[None, None] for member in gens] + [
        discs[0][None, None],
        discs[1][None, None],
        discs[2][None],
        verdict[None, None],
    ]
    return tuple(finals)


def solution(mesh):
    matrix = P("row", "col", None, None)
    return jax.shard_map(
        on_device,
        mesh=mesh,
        in_specs=(
            P("row", "col", None, None, None),
            matrix,
            matrix,
            P(),
            matrix,
            matrix,
            matrix,
            matrix,
            matrix,
            matrix,
            P("row", "col", None),
        ),
        out_specs=(
            matrix,
            matrix,
            matrix,
            matrix,
            matrix,
            matrix,
            P("row", "col", None),
            matrix,
        ),
        check_vma=False,
    )
```

```python
import functools

import jax
import jax.numpy as jnp
from jax import lax
from jax.experimental import pallas as pl
from jax.experimental.pallas import tpu as pltpu
from jax.sharding import PartitionSpec as P

STEPS = 2
LEARN_RATE = 0.05
BASE_RATE = 0.1
PACKET = 272
HEAD = 256
VMEM_LIMIT = 24 * 1024 * 1024
F32 = jnp.float32
BF16 = jnp.bfloat16


def dot(left, right):
    return jnp.dot(left, right, preferred_element_type=F32)


def dot_rows(left, right):
    return lax.dot_general(left, right, (((0,), (0,)), ((), ())), preferred_element_type=F32)


def silu_parts(half):
    above = 1.0 + jnp.tanh(half)
    value = half * above
    value_half = value.astype(BF16)
    above_half = above.astype(BF16)
    return value, value_half, above_half + value_half * (BF16(2.0) - above_half)


def silu_exact(half):
    above = 1.0 + jnp.tanh(half)
    value = half * above
    return value, above + value * (2.0 - above)


def sigmoid(value):
    return 0.5 * (1.0 + jnp.tanh(0.5 * value))


def split_two(value):
    high = value.astype(BF16)
    low = (value - high.astype(F32)).astype(BF16)
    return high, low


def shape(dims, dtype):
    return jax.ShapeDtypeStruct(dims, dtype)


def call(body, operands, out_shape, scratch=(), smem=(), hbm=(), flops=0):
    spaces = [pltpu.VMEM] * len(operands)
    for i in range(len(operands)):
        spaces[i] = pltpu.SMEM if i in smem else pltpu.HBM if i in hbm else pltpu.VMEM
    operands = [
        pltpu.with_memory_space_constraint(member, pltpu.HBM) if i in hbm else member
        for i, member in enumerate(operands)
    ]
    return pl.pallas_call(
        body,
        out_shape=tuple(out_shape),
        in_specs=[pl.BlockSpec(memory_space=space) for space in spaces],
        out_specs=tuple(pl.BlockSpec(memory_space=pltpu.VMEM) for _ in out_shape),
        scratch_shapes=list(scratch),
        compiler_params=pltpu.CompilerParams(vmem_limit_bytes=VMEM_LIMIT),
        cost_estimate=pl.CostEstimate(flops=flops, bytes_accessed=flops // 1000, transcendentals=0),
    )(*operands)


def start_all(pairs, semaphores):
    copies = [
        pltpu.make_async_copy(source, target, semaphores.at[i])
        for i, (source, target) in enumerate(pairs)
    ]
    for copy in copies:
        copy.start()
    return copies


def write_packet(packet_ref, one, two, rows):
    channels = one.shape[1]
    packet_ref[0:channels, :] = one.astype(BF16)
    packet_ref[channels:HEAD, :] = two.astype(BF16)
    spot = lax.broadcasted_iota(jnp.int32, (PACKET - HEAD, channels), 0)
    tail = jnp.zeros((PACKET - HEAD, channels), F32)
    for place, row in enumerate(rows):
        high, low = split_two(row)
        tail = jnp.where(spot == 2 * place, high.astype(F32), tail)
        tail = jnp.where(spot == 2 * place + 1, low.astype(F32), tail)
    packet_ref[HEAD:PACKET, :] = tail.astype(BF16)


def packet_row(tail, place):
    return tail[2 * place : 2 * place + 1, :] + tail[2 * place + 1 : 2 * place + 2, :]


def pack_body(one_hbm, two_hbm, out_hbm, packet_ref, one_ref, two_ref, out_ref, semaphores):
    pairs = [(one_hbm, one_ref), (two_hbm, two_ref), (out_hbm, out_ref)]
    for copy in start_all(pairs, semaphores):
        copy.wait()
    write_packet(packet_ref, one_ref[...], two_ref[...], [out_ref[...]])


def pack(params):
    outs = [shape((PACKET, params[0].shape[1]), BF16)] + [shape(m.shape, F32) for m in params]
    results = call(pack_body, params, outs, [pltpu.SemaphoreType.DMA((3,))], hbm=(0, 1, 2))
    return results[0], results[1:]


def dot_turned(left, right):
    return lax.dot_general(left, right, (((1,), (1,)), ((), ())), preferred_element_type=F32)


def unpack(packet_ref):
    channels = packet_ref.shape[1]
    tail = packet_ref[HEAD:PACKET, :].astype(F32)
    return packet_ref[0:channels, :], packet_ref[channels:HEAD, :], tail[0:1, :] + tail[1:2, :]


def both(left, right):
    blank = jnp.zeros_like(left)
    return jnp.concatenate(
        [jnp.concatenate([left, blank], axis=1), jnp.concatenate([blank, right], axis=1)], axis=0
    )


OFFSET = 2


def judge_steps(pair, result):
    images, one, two, out_row, shared = pair
    half = BF16(0.5)
    one_first = jnp.concatenate(one, axis=1) if shared else both(*one)
    halves = dot(images, one_first * half)
    yield
    _, first_half, slope_first = silu_parts(halves)
    image_half = 0.5 * images.astype(F32)
    if shared:
        image_half = twice(image_half)
    product = dot(first_half, both(*two) * half)
    yield
    feature, slope_out = silu_exact(image_half + product)
    sums = jnp.sum(feature.reshape(-1, 8, feature.shape[1]), axis=0)
    sums = jnp.sum(sums, axis=0, keepdims=True)
    outer = (0.5 * out_row) * slope_out
    outer_half = outer.astype(BF16)
    product = dot_turned(outer_half, both(*two) * half)
    yield
    inner_half = product.astype(BF16) * slope_first
    channels = inner_half.shape[1] // 2
    sides = [slice(0, channels), slice(channels, 2 * channels)]
    grad_two = [dot_rows(first_half[:, s], outer_half[:, s]) for s in sides]
    yield
    result.append((outer_half, inner_half))
    if shared:
        wide = dot_rows(images, inner_half)
        grad_one = [wide[:, s] for s in sides]
    else:
        grad_one = [dot_rows(images[:, s], inner_half[:, s]) for s in sides]
    for i, s in enumerate(sides):
        result.append((grad_one[i], grad_two[i], sums[:, s]))


def judge_pairs(pairs):
    results = [[] for _ in pairs]
    works = [judge_steps(pair, result) for pair, result in zip(pairs, results)]
    beat = 0
    left = set(range(len(works)))
    while left:
        for place in sorted(left):
            if beat >= place * OFFSET and next(works[place], True):
                left.discard(place)
        beat += 1
    return results


def verdict_lines(triples, out_rows, signs, places, lines_ref):
    lines_ref[...] = jnp.zeros_like(lines_ref)
    spot = lax.broadcasted_iota(jnp.int32, lines_ref.shape, 0)
    outs = jnp.zeros(lines_ref.shape, F32)
    is_fake = jnp.zeros(lines_ref.shape, jnp.bool_)
    for member, (triple, out_row) in enumerate(zip(triples, out_rows)):
        lines_ref[member : member + 1, :] = triple[2]
        outs = jnp.where(spot == member, out_row, outs)
        if signs[member]:
            is_fake = is_fake | (spot == member)
    features = lines_ref[...]
    scale = 1.0 / places
    verdicts = jnp.sum(features * outs, axis=1, keepdims=True) * scale
    verdicts = jnp.broadcast_to(verdicts, features.shape)
    plus = sigmoid(verdicts) * scale
    minus = -sigmoid(-verdicts) * scale
    return verdicts, minus, jnp.where(is_fake, plus, minus)


def weigh(triples, slopes):
    totals = None
    for triple, slope in zip(triples, slopes):
        parts = [slope * member for member in triple]
        totals = parts if totals is None else [x + y for x, y in zip(totals, parts)]
    return totals


def judge_own_body(step, batch, reals, packet_ref, fakes_ref, reals_ref, _, grads_ref, outer_ref, inner_ref, slope_ref, lines_ref):
    rows, channels = fakes_ref.shape
    places = rows // batch
    one, two, out_row = unpack(packet_ref)
    out_pair = twice(out_row)
    pairs = []
    for member in range(batch):
        span = slice(member * places, (member + 1) * places)
        images = jnp.concatenate([fakes_ref[span, :], reals_ref[step * reals + member]], axis=1)
        pairs.append((images, (one, one), (two, two), out_pair, False))
    results = judge_pairs(pairs)
    for member, result in enumerate(results):
        side = slice(member * channels, (member + 1) * channels)
        outer_ref[:, side] = result[0][0][:, 0:channels]
        inner_ref[:, side] = result[0][1][:, 0:channels]
    triples = [result[1] for result in results] + [result[2] for result in results]
    signs = [1] * batch + [0] * reals
    verdicts, minus, slopes = verdict_lines(triples, [out_row] * len(signs), signs, places, lines_ref)
    total_one, total_two, total_out = weigh(triples, [slopes[i : i + 1, :] for i in range(len(signs))])
    slope_ref[...] = minus
    grads_ref[0:channels, :] = total_one
    grads_ref[channels:HEAD, :] = total_two
    grads_ref[HEAD : HEAD + 8, :] = verdicts
    grads_ref[HEAD + 8 : PACKET, :] = jnp.broadcast_to(total_out, (8, channels))


def judge_own(packet, fakes, reals_rows, after, step, batch, reals):
    rows, channels = fakes.shape
    wide = (rows // batch, batch * channels)
    outs = [
        shape((PACKET, channels), F32),
        shape(wide, BF16),
        shape(wide, BF16),
        shape((8, channels), F32),
    ]
    body = functools.partial(judge_own_body, step, batch, reals)
    flops = 4 * 6 * 2 * 1024 * 128 * 128
    return call(body, [packet, fakes, reals_rows, after], outs, [pltpu.VMEM((8, channels), F32)], flops=flops)


def judge_others_body(judges, batch, *refs):
    refs = list(refs)
    packets = [refs.pop(0) for _ in range(judges)]
    fakes_ref = refs.pop(0)
    refs.pop(0)
    grads = [refs.pop(0) for _ in range(judges)]
    terms = [(refs.pop(0), refs.pop(0)) for _ in range(judges * batch // 2)]
    slope_ref = refs.pop(0)
    lines_ref = refs.pop(0)
    rows, channels = fakes_ref.shape
    places = rows // batch
    parts = [unpack(packet) for packet in packets]
    spans = [slice(member * places, (member + 1) * places) for member in range(batch)]
    pairs = []
    homes = []
    for which in range(0, judges, 2):
        ones, twos, outs = zip(*parts[which : which + 2])
        for member, span in enumerate(spans):
            pairs.append((fakes_ref[span, :], ones, twos, jnp.concatenate(outs, axis=1), True))
            homes.append(((which, member), (which + 1, member)))
    found = {}
    for result, home, (outer_ref, inner_ref) in zip(judge_pairs(pairs), homes, terms):
        outer_ref[...], inner_ref[...] = result[0]
        for side, key in enumerate(home):
            found[key] = result[1 + side]
    keys = sorted(found)
    triples = [found[key] for key in keys]
    out_rows = [parts[which][2] for which, _ in keys]
    verdicts, minus, slopes = verdict_lines(triples, out_rows, [1] * len(triples), places, lines_ref)
    slope_ref[...] = minus
    for which in range(judges):
        mine = range(which * batch, (which + 1) * batch)
        totals = weigh([triples[i] for i in mine], [slopes[i : i + 1, :] for i in mine])
        tail = [totals[2]] + [verdicts[i : i + 1, :] for i in mine]
        write_packet(grads[which], totals[0], totals[1], tail)


def judge_others(packets, fakes, batch, after):
    rows, channels = fakes.shape
    judges = len(packets)
    outs = [shape((PACKET, channels), BF16)] * judges
    outs = outs + [shape((rows // batch, 2 * channels), BF16)] * (judges * batch)
    outs = outs + [shape((8, channels), F32)]
    body = functools.partial(judge_others_body, judges, batch)
    scratch = [pltpu.VMEM((8, channels), F32)]
    flops = 2 * judges * 6 * 2 * 1024 * 128 * 128
    results = call(body, list(packets) + [fakes, after], outs, scratch, flops=flops)
    return results[:judges], results[judges:-1], results[-1]


def twice(tile):
    return jnp.concatenate([tile, tile], axis=1)


def gen_forward(latent, w_in, base, w_one, w_two, outs):
    fakes_ref, hidden_ref, middle_ref, gen_slope_ref, mid_slope_ref = outs
    places, channels = base.shape
    shifted = 0.5 * dot(latent.astype(BF16), w_in.astype(BF16))
    shift_row = jnp.concatenate([shifted[0:1, :], shifted[1:2, :]], axis=1)
    one = w_one.astype(BF16) * BF16(0.5)
    two = w_two.astype(BF16)
    _, hidden_half, slope_gen = silu_parts(twice(0.5 * base.astype(BF16).astype(F32)) + shift_row)
    _, middle_half, slope_mid = silu_parts(dot(hidden_half, both(one, one)))
    fakes = (hidden_half.astype(F32) + dot(middle_half, both(two, two))).astype(BF16)
    fakes_ref[0:places, :] = fakes[:, 0:channels]
    fakes_ref[places : 2 * places, :] = fakes[:, channels : 2 * channels]
    hidden_ref[...] = hidden_half
    middle_ref[...] = middle_half
    gen_slope_ref[...] = slope_gen
    mid_slope_ref[...] = slope_mid


def stored_shapes(places, channels):
    wide = (places, 2 * channels)
    return [
        shape((2 * places, channels), BF16),
        shape(wide, BF16),
        shape(wide, BF16),
        shape(wide, BF16),
        shape(wide, BF16),
    ]


def begin_body(batch, reals, seed_hbm, index_hbm, *refs):
    bank, data, *weights = refs[:6]
    weight_refs = refs[6:10]
    latent_ref, reals_ref = refs[10:12]
    outs = refs[12:17]
    bank_ref, seed_ref, index_ref, semaphores = refs[17:]
    count = len(weights) + 3
    pairs = [(seed_hbm, seed_ref), (index_hbm, index_ref), (bank, bank_ref)]
    copies = start_all(pairs + list(zip(weights, weight_refs)), semaphores)
    latent_ref[...] = jnp.zeros_like(latent_ref)
    for copy in copies[:2]:
        copy.wait()
    late = []
    for step in range(STEPS):
        for member in range(reals):
            late.append((data.at[index_ref[step, member]], reals_ref.at[step * reals + member]))
    late = start_all(late, semaphores.at[pl.ds(count, len(late))])
    for copy in copies[2:]:
        copy.wait()
    for step in range(STEPS):
        for member in range(batch):
            row = bank_ref[pl.ds(seed_ref[step, member], 1), :]
            latent_ref[step, member : member + 1, :] = row.astype(BF16).astype(F32)
    w_in, base, w_one, w_two = [ref[...] for ref in weight_refs]
    gen_forward(latent_ref[0], w_in, base, w_one, w_two, outs)
    for copy in late:
        copy.wait()


def begin(seed, index, bank, data, weights):
    batch = seed.shape[1]
    reals = index.shape[1]
    places, channels = weights[1].shape
    outs = [shape(member.shape, F32) for member in weights]
    outs = outs + [shape((STEPS, 8, channels), F32), shape((STEPS * reals, places, channels), BF16)]
    outs = outs + stored_shapes(places, channels)
    scratch = [
        pltpu.VMEM(bank.shape, F32),
        pltpu.SMEM(seed.shape, jnp.int32),
        pltpu.SMEM(index.shape, jnp.int32),
        pltpu.SemaphoreType.DMA((len(weights) + 3 + STEPS * reals,)),
    ]
    operands = [seed, index, bank, data] + list(weights)
    body = functools.partial(begin_body, batch, reals)
    flops = 4 * 2 * 1024 * 128 * 128
    results = call(body, operands, outs, scratch, hbm=range(8), flops=flops)
    return results[:4], results[4], results[5], results[6:]


def gen_back_body(step, judges, batch, *refs):
    is_last = step == STEPS - 1
    refs = list(refs)
    packets = [refs.pop(0) for _ in range(1 + judges)]
    own_terms = [refs.pop(0) for _ in range(2)]
    terms = [(refs.pop(0), refs.pop(0)) for _ in range(judges * batch // 2)]
    own_slope, slope_ref = [refs.pop(0) for _ in range(2)]
    hidden_ref, middle_ref, gen_slope_ref, mid_slope_ref, latent_ref = [refs.pop(0) for _ in range(5)]
    in_ref, base_ref, one_ref, two_ref = [refs.pop(0) for _ in range(4)]
    new_in, new_base, new_one, new_two = [refs.pop(0) for _ in range(4)]
    places, channels = base_ref.shape
    sides = (slice(0, channels), slice(channels, 2 * channels))

    def weighed(pair, ones, lines):
        outer, inner = pair
        unit = outer[...].astype(F32) + dot_turned(inner[...], both(*ones))
        return unit * jnp.concatenate(lines, axis=1)

    ones = [packet[0:channels, :] for packet in packets]
    own_lines = [own_slope[member : member + 1, :] for member in range(batch)]
    cotangent = weighed(own_terms, (ones[0], ones[0]), own_lines)
    halves = [None] * batch
    places_left = iter(terms)
    for which in range(0, judges, 2):
        for member in range(batch):
            lines = []
            for judge in (which, which + 1):
                place = judge * batch + member
                lines.append(slope_ref[place : place + 1, :])
            part = weighed(next(places_left), (ones[1 + which], ones[2 + which]), lines)
            part = part[:, sides[0]] + part[:, sides[1]]
            halves[member] = part if halves[member] is None else halves[member] + part
    cotangent = cotangent + jnp.concatenate(halves, axis=1)
    cotangent_half = cotangent.astype(BF16)
    one = one_ref[...].astype(BF16)
    two = two_ref[...].astype(BF16) * BF16(0.5)
    inner_half = (dot_turned(cotangent_half, both(two, two)).astype(BF16) * mid_slope_ref[...])
    outer = (cotangent + dot_turned(inner_half, both(one, one))) * gen_slope_ref[...].astype(F32)
    grad_two = [dot_rows(middle_ref[:, side], cotangent_half[:, side]) for side in sides]
    grad_one = [dot_rows(hidden_ref[:, side], inner_half[:, side]) for side in sides]
    sums = jnp.sum(jnp.sum(outer.reshape(-1, 8, 2 * channels), axis=0), axis=0, keepdims=True)
    latent_turned = latent_ref[step].T
    grad_in = [
        latent_turned[:, member : member + 1] * (0.5 * sums[:, side])
        for member, side in enumerate(sides)
    ]
    base = base_ref[...] - (0.5 * BASE_RATE * places) * (outer[:, sides[0]] + outer[:, sides[1]])
    w_one = one_ref[...] - LEARN_RATE * (grad_one[0] + grad_one[1])
    w_two = two_ref[...] - LEARN_RATE * (grad_two[0] + grad_two[1])
    w_in = in_ref[...] - LEARN_RATE * (grad_in[0] + grad_in[1])
    new_in[...] = w_in
    new_base[...] = base
    new_one[...] = w_one
    new_two[...] = w_two
    if not is_last:
        gen_forward(latent_ref[step + 1], w_in, base, w_one, w_two, refs)


def gen_back(step, packets, own_terms, terms, slopes, stored, latents, weights):
    places, channels = weights[1].shape
    batch = stored[0].shape[0] // places
    operands = list(packets) + list(own_terms) + list(terms) + list(slopes)
    operands = operands + list(stored[1:]) + [latents] + list(weights)
    outs = [shape(member.shape, F32) for member in weights]
    if step < STEPS - 1:
        outs = outs + stored_shapes(places, channels)
    body = functools.partial(gen_back_body, step, len(packets) - 1, batch)
    flops = 24 * 2 * 1024 * 128 * 128
    results = call(body, operands, outs, flops=flops)
    return results[:4], results[4:]


def disc_update_body(batch, reals, is_last, grads_ref, *refs):
    refs = list(refs)
    returns = [refs.pop(0) for _ in range(4)]
    refs.pop(0)
    params = [refs.pop(0) for _ in range(3)]
    before = refs.pop(0) if is_last else None
    news = [refs.pop(0) for _ in range(3)]
    last_ref = refs.pop(0)
    channels = params[0].shape[0]
    one = grads_ref[0:channels, :]
    two = grads_ref[channels:HEAD, :]
    out = grads_ref[HEAD + 8 : HEAD + 9, :]
    verdicts = [grads_ref[HEAD + i : HEAD + 1 + i, :] for i in range(batch + reals)]
    tails = []
    for back in returns:
        one = one + back[0:channels, :].astype(F32)
        two = two + back[channels:HEAD, :].astype(F32)
        tail = back[HEAD:PACKET, :].astype(F32)
        out = out + packet_row(tail, 0)
        tails.append([packet_row(tail, 1 + i) for i in range(batch)])
    ordered = verdicts[:batch]
    for axis, (inner, outer) in (("row", (tails[2], tails[1])), ("col", (tails[3], tails[0]))):
        is_odd = lax.rem(lax.axis_index(axis), 2) == 1
        ordered = ordered + [jnp.where(is_odd, a, b) for a, b in zip(inner, outer)]
        ordered = ordered + [jnp.where(is_odd, b, a) for a, b in zip(inner, outer)]
    ordered = ordered + verdicts[batch:]
    updated = [member[...] - LEARN_RATE * grad for member, grad in zip(params, (one, two, out))]
    for new, value in zip(news, updated):
        new[...] = value
    lanes = lax.broadcasted_iota(jnp.int32, (1, channels), 1)
    line = jnp.zeros((1, channels), F32)
    for place, value in enumerate(ordered):
        line = jnp.where(lanes == place, value, line)
    count = len(ordered)
    if is_last:
        last_ref[0:1, :] = before[0:1, 0:count]
        last_ref[1:2, :] = line[:, 0:count]
    else:
        last_ref[...] = line
        write_packet(refs[0], updated[0], updated[1], [updated[2]])


def disc_update(grads, returns, after, params, before, batch, reals):
    is_last = before is not None
    operands = [grads] + list(returns) + [after] + list(params) + ([before] if is_last else [])
    outs = [shape(member.shape, F32) for member in params]
    if is_last:
        outs = outs + [shape((STEPS, 5 * batch + reals), F32)]
    else:
        outs = outs + [shape((1, 128), F32), shape((PACKET, 128), BF16)]
    body = functools.partial(disc_update_body, batch, reals, is_last)
    return call(body, operands, outs, hbm=(5,) if is_last else ())


def paired(block, axis, offset):
    count = lax.axis_size(axis)
    route = []
    for i in range(0, count, 2):
        first, second = (i + offset) % count, (i + offset + 1) % count
        route += [(first, second), (second, first)]
    return lax.ppermute(block, axis, route)


EDGES = (("col", 1), ("row", 1), ("row", 0), ("col", 0))


def on_device(
    data, real_index, latent_seed, latent_bank, g_in, g_base, g_one, g_two, d_one, d_two, d_out
):
    batch = latent_seed.shape[3]
    reals = real_index.shape[3]
    packet, discs = pack([d_one[0, 0], d_two[0, 0], d_out[0]])
    verdict = None
    for step in range(STEPS):
        is_last = step == STEPS - 1
        arrived = [paired(packet, axis, offset) for axis, offset in EDGES]
        if step == 0:
            gens, latents, reals_rows, stored = begin(
                latent_seed[0, 0],
                real_index[0, 0],
                latent_bank,
                data[0, 0],
                [member[0, 0] for member in (g_in, g_base, g_one, g_two)],
            )
        fakes = stored[0]
        own_grads, *own_terms, own_slope = judge_own(
            packet, fakes, reals_rows, stored[1], step, batch, reals
        )
        grads, terms, slope = judge_others(arrived, fakes, batch, own_slope)
        returns = [paired(grad, *edge) for grad, edge in zip(grads, EDGES)]
        gens, stored = gen_back(
            step, [packet] + arrived, own_terms, terms, [own_slope, slope], stored, latents, gens
        )
        results = disc_update(
            own_grads, returns, gens[0], discs, verdict if is_last else None, batch, reals
        )
        discs = results[:3]
        verdict = results[3]
        packet = None if is_last else results[4]
    finals = [member[None, None] for member in gens] + [
        discs[0][None, None],
        discs[1][None, None],
        discs[2][None],
        verdict[None, None],
    ]
    return tuple(finals)


def solution(mesh):
    matrix = P("row", "col", None, None)
    return jax.shard_map(
        on_device,
        mesh=mesh,
        in_specs=(
            P("row", "col", None, None, None),
            matrix,
            matrix,
            P(),
            matrix,
            matrix,
            matrix,
            matrix,
            matrix,
            matrix,
            P("row", "col", None),
        ),
        out_specs=(
            matrix,
            matrix,
            matrix,
            matrix,
            matrix,
            matrix,
            P("row", "col", None),
            matrix,
        ),
        check_vma=False,
    )
```

```python
import functools

import jax
import jax.numpy as jnp
from jax import lax
from jax.experimental import pallas as pl
from jax.experimental.pallas import tpu as pltpu
from jax.sharding import PartitionSpec as P

STEPS = 2
LEARN_RATE = 0.05
BASE_RATE = 0.1
PACKET = 272
HEAD = 256
VMEM_LIMIT = 24 * 1024 * 1024
F32 = jnp.float32
BF16 = jnp.bfloat16


def dot(left, right):
    return jnp.dot(left, right, preferred_element_type=F32)


def dot_rows(left, right):
    return lax.dot_general(left, right, (((0,), (0,)), ((), ())), preferred_element_type=F32)


def silu_parts(half):
    above = 1.0 + jnp.tanh(half)
    value = half * above
    value_half = value.astype(BF16)
    above_half = above.astype(BF16)
    return value, value_half, above_half + value_half * (BF16(2.0) - above_half)


def silu_exact(half):
    above = 1.0 + jnp.tanh(half)
    value = half * above
    return value, above + value * (2.0 - above)


def sigmoid(value):
    return 0.5 * (1.0 + jnp.tanh(0.5 * value))


def split_two(value):
    high = value.astype(BF16)
    low = (value - high.astype(F32)).astype(BF16)
    return high, low


def shape(dims, dtype):
    return jax.ShapeDtypeStruct(dims, dtype)


def call(body, operands, out_shape, scratch=(), smem=(), hbm=(), flops=0):
    spaces = [pltpu.VMEM] * len(operands)
    for i in range(len(operands)):
        spaces[i] = pltpu.SMEM if i in smem else pltpu.HBM if i in hbm else pltpu.VMEM
    operands = [
        pltpu.with_memory_space_constraint(member, pltpu.HBM) if i in hbm else member
        for i, member in enumerate(operands)
    ]
    return pl.pallas_call(
        body,
        out_shape=tuple(out_shape),
        in_specs=[pl.BlockSpec(memory_space=space) for space in spaces],
        out_specs=tuple(pl.BlockSpec(memory_space=pltpu.VMEM) for _ in out_shape),
        scratch_shapes=list(scratch),
        compiler_params=pltpu.CompilerParams(vmem_limit_bytes=VMEM_LIMIT),
        cost_estimate=pl.CostEstimate(flops=flops, bytes_accessed=flops // 1000, transcendentals=0),
    )(*operands)


def start_all(pairs, semaphores):
    copies = [
        pltpu.make_async_copy(source, target, semaphores.at[i])
        for i, (source, target) in enumerate(pairs)
    ]
    for copy in copies:
        copy.start()
    return copies


def write_packet(packet_ref, one, two, rows):
    channels = one.shape[1]
    packet_ref[0:channels, :] = one.astype(BF16)
    packet_ref[channels:HEAD, :] = two.astype(BF16)
    spot = lax.broadcasted_iota(jnp.int32, (PACKET - HEAD, channels), 0)
    tail = jnp.zeros((PACKET - HEAD, channels), F32)
    for place, row in enumerate(rows):
        high, low = split_two(row)
        tail = jnp.where(spot == 2 * place, high.astype(F32), tail)
        tail = jnp.where(spot == 2 * place + 1, low.astype(F32), tail)
    packet_ref[HEAD:PACKET, :] = tail.astype(BF16)


def packet_row(tail, place):
    return tail[2 * place : 2 * place + 1, :] + tail[2 * place + 1 : 2 * place + 2, :]


def pack_body(one_hbm, two_hbm, out_hbm, packet_ref, one_ref, two_ref, out_ref, semaphores):
    pairs = [(one_hbm, one_ref), (two_hbm, two_ref), (out_hbm, out_ref)]
    for copy in start_all(pairs, semaphores):
        copy.wait()
    write_packet(packet_ref, one_ref[...], two_ref[...], [out_ref[...]])


def pack(params):
    outs = [shape((PACKET, params[0].shape[1]), BF16)] + [shape(m.shape, F32) for m in params]
    results = call(pack_body, params, outs, [pltpu.SemaphoreType.DMA((3,))], hbm=(0, 1, 2))
    return results[0], results[1:]


def dot_turned(left, right):
    return lax.dot_general(left, right, (((1,), (1,)), ((), ())), preferred_element_type=F32)


def unpack(packet_ref):
    channels = packet_ref.shape[1]
    tail = packet_ref[HEAD:PACKET, :].astype(F32)
    return packet_ref[0:channels, :], packet_ref[channels:HEAD, :], tail[0:1, :] + tail[1:2, :]


def both(left, right):
    blank = jnp.zeros_like(left)
    return jnp.concatenate(
        [jnp.concatenate([left, blank], axis=1), jnp.concatenate([blank, right], axis=1)], axis=0
    )


OFFSET = 2


def judge_steps(pair, result):
    images, one, two, out_row, shared = pair
    half = BF16(0.5)
    one_first = jnp.concatenate(one, axis=1) if shared else both(*one)
    halves = dot(images, one_first * half)
    yield
    _, first_half, slope_first = silu_parts(halves)
    image_half = 0.5 * images.astype(F32)
    if shared:
        image_half = twice(image_half)
    product = dot(first_half, both(*two) * half)
    yield
    feature, slope_out = silu_exact(image_half + product)
    sums = jnp.sum(feature.reshape(-1, 8, feature.shape[1]), axis=0)
    sums = jnp.sum(sums, axis=0, keepdims=True)
    outer = (0.5 * out_row) * slope_out
    outer_half = outer.astype(BF16)
    product = dot_turned(outer_half, both(*two) * half)
    yield
    inner_half = product.astype(BF16) * slope_first
    channels = inner_half.shape[1] // 2
    sides = [slice(0, channels), slice(channels, 2 * channels)]
    square = dot_rows(first_half, outer_half)
    grad_two = [square[s, s] for s in sides]
    yield
    result.append((outer_half, inner_half))
    wide = dot_rows(images, inner_half)
    grad_one = [wide[:, s] if shared else wide[s, s] for s in sides]
    for i, s in enumerate(sides):
        result.append((grad_one[i], grad_two[i], sums[:, s]))


def judge_pairs(pairs):
    results = [[] for _ in pairs]
    works = [judge_steps(pair, result) for pair, result in zip(pairs, results)]
    beat = 0
    left = set(range(len(works)))
    while left:
        for place in sorted(left):
            if beat >= place * OFFSET and next(works[place], True):
                left.discard(place)
        beat += 1
    return results


def verdict_lines(triples, out_rows, signs, places, lines_ref):
    lines_ref[...] = jnp.zeros_like(lines_ref)
    spot = lax.broadcasted_iota(jnp.int32, lines_ref.shape, 0)
    outs = jnp.zeros(lines_ref.shape, F32)
    is_fake = jnp.zeros(lines_ref.shape, jnp.bool_)
    for member, (triple, out_row) in enumerate(zip(triples, out_rows)):
        lines_ref[member : member + 1, :] = triple[2]
        outs = jnp.where(spot == member, out_row, outs)
        if signs[member]:
            is_fake = is_fake | (spot == member)
    features = lines_ref[...]
    scale = 1.0 / places
    verdicts = jnp.sum(features * outs, axis=1, keepdims=True) * scale
    verdicts = jnp.broadcast_to(verdicts, features.shape)
    plus = sigmoid(verdicts) * scale
    minus = -sigmoid(-verdicts) * scale
    return verdicts, minus, jnp.where(is_fake, plus, minus)


def weigh(triples, slopes):
    totals = None
    for triple, slope in zip(triples, slopes):
        parts = [slope * member for member in triple]
        totals = parts if totals is None else [x + y for x, y in zip(totals, parts)]
    return totals


def judge_own_body(step, batch, reals, packet_ref, fakes_ref, reals_ref, _, grads_ref, outer_ref, inner_ref, slope_ref, lines_ref):
    rows, channels = fakes_ref.shape
    places = rows // batch
    one, two, out_row = unpack(packet_ref)
    out_pair = twice(out_row)
    pairs = []
    for member in range(batch):
        span = slice(member * places, (member + 1) * places)
        images = jnp.concatenate([fakes_ref[span, :], reals_ref[step * reals + member]], axis=1)
        pairs.append((images, (one, one), (two, two), out_pair, False))
    results = judge_pairs(pairs)
    for member, result in enumerate(results):
        side = slice(member * channels, (member + 1) * channels)
        outer_ref[:, side] = result[0][0][:, 0:channels]
        inner_ref[:, side] = result[0][1][:, 0:channels]
    triples = [result[1] for result in results] + [result[2] for result in results]
    signs = [1] * batch + [0] * reals
    verdicts, minus, slopes = verdict_lines(triples, [out_row] * len(signs), signs, places, lines_ref)
    total_one, total_two, total_out = weigh(triples, [slopes[i : i + 1, :] for i in range(len(signs))])
    slope_ref[...] = minus
    grads_ref[0:channels, :] = total_one
    grads_ref[channels:HEAD, :] = total_two
    grads_ref[HEAD : HEAD + 8, :] = verdicts
    grads_ref[HEAD + 8 : PACKET, :] = jnp.broadcast_to(total_out, (8, channels))


def judge_own(packet, fakes, reals_rows, after, step, batch, reals):
    rows, channels = fakes.shape
    wide = (rows // batch, batch * channels)
    outs = [
        shape((PACKET, channels), F32),
        shape(wide, BF16),
        shape(wide, BF16),
        shape((8, channels), F32),
    ]
    body = functools.partial(judge_own_body, step, batch, reals)
    flops = 4 * 6 * 2 * 1024 * 128 * 128
    return call(body, [packet, fakes, reals_rows, after], outs, [pltpu.VMEM((8, channels), F32)], flops=flops)


def judge_others_body(judges, batch, *refs):
    refs = list(refs)
    packets = [refs.pop(0) for _ in range(judges)]
    fakes_ref = refs.pop(0)
    refs.pop(0)
    grads = [refs.pop(0) for _ in range(judges)]
    terms = [(refs.pop(0), refs.pop(0)) for _ in range(judges * batch // 2)]
    slope_ref = refs.pop(0)
    lines_ref = refs.pop(0)
    rows, channels = fakes_ref.shape
    places = rows // batch
    parts = [unpack(packet) for packet in packets]
    spans = [slice(member * places, (member + 1) * places) for member in range(batch)]
    pairs = []
    homes = []
    for which in range(0, judges, 2):
        ones, twos, outs = zip(*parts[which : which + 2])
        for member, span in enumerate(spans):
            pairs.append((fakes_ref[span, :], ones, twos, jnp.concatenate(outs, axis=1), True))
            homes.append(((which, member), (which + 1, member)))
    found = {}
    for result, home, (outer_ref, inner_ref) in zip(judge_pairs(pairs), homes, terms):
        outer_ref[...], inner_ref[...] = result[0]
        for side, key in enumerate(home):
            found[key] = result[1 + side]
    keys = sorted(found)
    triples = [found[key] for key in keys]
    out_rows = [parts[which][2] for which, _ in keys]
    verdicts, minus, slopes = verdict_lines(triples, out_rows, [1] * len(triples), places, lines_ref)
    slope_ref[...] = minus
    for which in range(judges):
        mine = range(which * batch, (which + 1) * batch)
        totals = weigh([triples[i] for i in mine], [slopes[i : i + 1, :] for i in mine])
        tail = [totals[2]] + [verdicts[i : i + 1, :] for i in mine]
        write_packet(grads[which], totals[0], totals[1], tail)


def judge_others(packets, fakes, batch, after):
    rows, channels = fakes.shape
    judges = len(packets)
    outs = [shape((PACKET, channels), BF16)] * judges
    outs = outs + [shape((rows // batch, 2 * channels), BF16)] * (judges * batch)
    outs = outs + [shape((8, channels), F32)]
    body = functools.partial(judge_others_body, judges, batch)
    scratch = [pltpu.VMEM((8, channels), F32)]
    flops = 2 * judges * 6 * 2 * 1024 * 128 * 128
    results = call(body, list(packets) + [fakes, after], outs, scratch, flops=flops)
    return results[:judges], results[judges:-1], results[-1]


def twice(tile):
    return jnp.concatenate([tile, tile], axis=1)


def gen_forward(latent, w_in, base, w_one, w_two, outs):
    fakes_ref, hidden_ref, middle_ref, gen_slope_ref, mid_slope_ref = outs
    places, channels = base.shape
    shifted = 0.5 * dot(latent.astype(BF16), w_in.astype(BF16))
    shift_row = jnp.concatenate([shifted[0:1, :], shifted[1:2, :]], axis=1)
    one = w_one.astype(BF16) * BF16(0.5)
    two = w_two.astype(BF16)
    _, hidden_half, slope_gen = silu_parts(twice(0.5 * base.astype(BF16).astype(F32)) + shift_row)
    _, middle_half, slope_mid = silu_parts(dot(hidden_half, both(one, one)))
    fakes = (hidden_half.astype(F32) + dot(middle_half, both(two, two))).astype(BF16)
    fakes_ref[0:places, :] = fakes[:, 0:channels]
    fakes_ref[places : 2 * places, :] = fakes[:, channels : 2 * channels]
    hidden_ref[...] = hidden_half
    middle_ref[...] = middle_half
    gen_slope_ref[...] = slope_gen
    mid_slope_ref[...] = slope_mid


def stored_shapes(places, channels):
    wide = (places, 2 * channels)
    return [
        shape((2 * places, channels), BF16),
        shape(wide, BF16),
        shape(wide, BF16),
        shape(wide, BF16),
        shape(wide, BF16),
    ]


def begin_body(batch, reals, seed_hbm, index_hbm, *refs):
    bank, data, *weights = refs[:6]
    weight_refs = refs[6:10]
    latent_ref, reals_ref = refs[10:12]
    outs = refs[12:17]
    bank_ref, seed_ref, index_ref, semaphores = refs[17:]
    count = len(weights) + 3
    pairs = [(seed_hbm, seed_ref), (index_hbm, index_ref), (bank, bank_ref)]
    copies = start_all(pairs + list(zip(weights, weight_refs)), semaphores)
    latent_ref[...] = jnp.zeros_like(latent_ref)
    for copy in copies[:2]:
        copy.wait()
    late = []
    for step in range(STEPS):
        for member in range(reals):
            late.append((data.at[index_ref[step, member]], reals_ref.at[step * reals + member]))
    late = start_all(late, semaphores.at[pl.ds(count, len(late))])
    for copy in copies[2:]:
        copy.wait()
    for step in range(STEPS):
        for member in range(batch):
            row = bank_ref[pl.ds(seed_ref[step, member], 1), :]
            latent_ref[step, member : member + 1, :] = row.astype(BF16).astype(F32)
    w_in, base, w_one, w_two = [ref[...] for ref in weight_refs]
    gen_forward(latent_ref[0], w_in, base, w_one, w_two, outs)
    for copy in late:
        copy.wait()


def begin(seed, index, bank, data, weights):
    batch = seed.shape[1]
    reals = index.shape[1]
    places, channels = weights[1].shape
    outs = [shape(member.shape, F32) for member in weights]
    outs = outs + [shape((STEPS, 8, channels), F32), shape((STEPS * reals, places, channels), BF16)]
    outs = outs + stored_shapes(places, channels)
    scratch = [
        pltpu.VMEM(bank.shape, F32),
        pltpu.SMEM(seed.shape, jnp.int32),
        pltpu.SMEM(index.shape, jnp.int32),
        pltpu.SemaphoreType.DMA((len(weights) + 3 + STEPS * reals,)),
    ]
    operands = [seed, index, bank, data] + list(weights)
    body = functools.partial(begin_body, batch, reals)
    flops = 4 * 2 * 1024 * 128 * 128
    results = call(body, operands, outs, scratch, hbm=range(8), flops=flops)
    return results[:4], results[4], results[5], results[6:]


def gen_back_body(step, judges, batch, *refs):
    is_last = step == STEPS - 1
    refs = list(refs)
    packets = [refs.pop(0) for _ in range(1 + judges)]
    own_terms = [refs.pop(0) for _ in range(2)]
    terms = [(refs.pop(0), refs.pop(0)) for _ in range(judges * batch // 2)]
    own_slope, slope_ref = [refs.pop(0) for _ in range(2)]
    hidden_ref, middle_ref, gen_slope_ref, mid_slope_ref, latent_ref = [refs.pop(0) for _ in range(5)]
    in_ref, base_ref, one_ref, two_ref = [refs.pop(0) for _ in range(4)]
    new_in, new_base, new_one, new_two = [refs.pop(0) for _ in range(4)]
    places, channels = base_ref.shape
    sides = (slice(0, channels), slice(channels, 2 * channels))

    def weighed(pair, ones, lines):
        outer, inner = pair
        unit = outer[...].astype(F32) + dot_turned(inner[...], both(*ones))
        return unit * jnp.concatenate(lines, axis=1)

    ones = [packet[0:channels, :] for packet in packets]
    own_lines = [own_slope[member : member + 1, :] for member in range(batch)]
    cotangent = weighed(own_terms, (ones[0], ones[0]), own_lines)
    halves = [None] * batch
    places_left = iter(terms)
    for which in range(0, judges, 2):
        for member in range(batch):
            lines = []
            for judge in (which, which + 1):
                place = judge * batch + member
                lines.append(slope_ref[place : place + 1, :])
            part = weighed(next(places_left), (ones[1 + which], ones[2 + which]), lines)
            part = part[:, sides[0]] + part[:, sides[1]]
            halves[member] = part if halves[member] is None else halves[member] + part
    cotangent = cotangent + jnp.concatenate(halves, axis=1)
    cotangent_half = cotangent.astype(BF16)
    one = one_ref[...].astype(BF16)
    two = two_ref[...].astype(BF16) * BF16(0.5)
    inner_half = (dot_turned(cotangent_half, both(two, two)).astype(BF16) * mid_slope_ref[...])
    outer = (cotangent + dot_turned(inner_half, both(one, one))) * gen_slope_ref[...].astype(F32)
    square_two = dot_rows(middle_ref[...], cotangent_half)
    square_one = dot_rows(hidden_ref[...], inner_half)
    grad_two = [square_two[side, side] for side in sides]
    grad_one = [square_one[side, side] for side in sides]
    sums = jnp.sum(jnp.sum(outer.reshape(-1, 8, 2 * channels), axis=0), axis=0, keepdims=True)
    latent_turned = latent_ref[step].T
    grad_in = [
        latent_turned[:, member : member + 1] * (0.5 * sums[:, side])
        for member, side in enumerate(sides)
    ]
    base = base_ref[...] - (0.5 * BASE_RATE * places) * (outer[:, sides[0]] + outer[:, sides[1]])
    w_one = one_ref[...] - LEARN_RATE * (grad_one[0] + grad_one[1])
    w_two = two_ref[...] - LEARN_RATE * (grad_two[0] + grad_two[1])
    w_in = in_ref[...] - LEARN_RATE * (grad_in[0] + grad_in[1])
    new_in[...] = w_in
    new_base[...] = base
    new_one[...] = w_one
    new_two[...] = w_two
    if not is_last:
        gen_forward(latent_ref[step + 1], w_in, base, w_one, w_two, refs)


def gen_back(step, packets, own_terms, terms, slopes, stored, latents, weights):
    places, channels = weights[1].shape
    batch = stored[0].shape[0] // places
    operands = list(packets) + list(own_terms) + list(terms) + list(slopes)
    operands = operands + list(stored[1:]) + [latents] + list(weights)
    outs = [shape(member.shape, F32) for member in weights]
    if step < STEPS - 1:
        outs = outs + stored_shapes(places, channels)
    body = functools.partial(gen_back_body, step, len(packets) - 1, batch)
    flops = 24 * 2 * 1024 * 128 * 128
    results = call(body, operands, outs, flops=flops)
    return results[:4], results[4:]


def disc_update_body(batch, reals, is_last, grads_ref, *refs):
    refs = list(refs)
    returns = [refs.pop(0) for _ in range(4)]
    refs.pop(0)
    params = [refs.pop(0) for _ in range(3)]
    before = refs.pop(0) if is_last else None
    news = [refs.pop(0) for _ in range(3)]
    last_ref = refs.pop(0)
    channels = params[0].shape[0]
    one = grads_ref[0:channels, :]
    two = grads_ref[channels:HEAD, :]
    out = grads_ref[HEAD + 8 : HEAD + 9, :]
    verdicts = [grads_ref[HEAD + i : HEAD + 1 + i, :] for i in range(batch + reals)]
    tails = []
    for back in returns:
        one = one + back[0:channels, :].astype(F32)
        two = two + back[channels:HEAD, :].astype(F32)
        tail = back[HEAD:PACKET, :].astype(F32)
        out = out + packet_row(tail, 0)
        tails.append([packet_row(tail, 1 + i) for i in range(batch)])
    ordered = verdicts[:batch]
    for axis, (inner, outer) in (("row", (tails[2], tails[1])), ("col", (tails[3], tails[0]))):
        is_odd = lax.rem(lax.axis_index(axis), 2) == 1
        ordered = ordered + [jnp.where(is_odd, a, b) for a, b in zip(inner, outer)]
        ordered = ordered + [jnp.where(is_odd, b, a) for a, b in zip(inner, outer)]
    ordered = ordered + verdicts[batch:]
    updated = [member[...] - LEARN_RATE * grad for member, grad in zip(params, (one, two, out))]
    for new, value in zip(news, updated):
        new[...] = value
    lanes = lax.broadcasted_iota(jnp.int32, (1, channels), 1)
    line = jnp.zeros((1, channels), F32)
    for place, value in enumerate(ordered):
        line = jnp.where(lanes == place, value, line)
    count = len(ordered)
    if is_last:
        last_ref[0:1, :] = before[0:1, 0:count]
        last_ref[1:2, :] = line[:, 0:count]
    else:
        last_ref[...] = line
        write_packet(refs[0], updated[0], updated[1], [updated[2]])


def disc_update(grads, returns, after, params, before, batch, reals):
    is_last = before is not None
    operands = [grads] + list(returns) + [after] + list(params) + ([before] if is_last else [])
    outs = [shape(member.shape, F32) for member in params]
    if is_last:
        outs = outs + [shape((STEPS, 5 * batch + reals), F32)]
    else:
        outs = outs + [shape((1, 128), F32), shape((PACKET, 128), BF16)]
    body = functools.partial(disc_update_body, batch, reals, is_last)
    return call(body, operands, outs, hbm=(5,) if is_last else ())


def paired(block, axis, offset):
    count = lax.axis_size(axis)
    route = []
    for i in range(0, count, 2):
        first, second = (i + offset) % count, (i + offset + 1) % count
        route += [(first, second), (second, first)]
    return lax.ppermute(block, axis, route)


EDGES = (("col", 1), ("row", 1), ("row", 0), ("col", 0))


def on_device(
    data, real_index, latent_seed, latent_bank, g_in, g_base, g_one, g_two, d_one, d_two, d_out
):
    batch = latent_seed.shape[3]
    reals = real_index.shape[3]
    packet, discs = pack([d_one[0, 0], d_two[0, 0], d_out[0]])
    verdict = None
    for step in range(STEPS):
        is_last = step == STEPS - 1
        arrived = [paired(packet, axis, offset) for axis, offset in EDGES]
        if step == 0:
            gens, latents, reals_rows, stored = begin(
                latent_seed[0, 0],
                real_index[0, 0],
                latent_bank,
                data[0, 0],
                [member[0, 0] for member in (g_in, g_base, g_one, g_two)],
            )
        fakes = stored[0]
        own_grads, *own_terms, own_slope = judge_own(
            packet, fakes, reals_rows, stored[1], step, batch, reals
        )
        grads, terms, slope = judge_others(arrived, fakes, batch, own_slope)
        returns = [paired(grad, *edge) for grad, edge in zip(grads, EDGES)]
        gens, stored = gen_back(
            step, [packet] + arrived, own_terms, terms, [own_slope, slope], stored, latents, gens
        )
        results = disc_update(
            own_grads, returns, gens[0], discs, verdict if is_last else None, batch, reals
        )
        discs = results[:3]
        verdict = results[3]
        packet = None if is_last else results[4]
    finals = [member[None, None] for member in gens] + [
        discs[0][None, None],
        discs[1][None, None],
        discs[2][None],
        verdict[None, None],
    ]
    return tuple(finals)


def solution(mesh):
    matrix = P("row", "col", None, None)
    return jax.shard_map(
        on_device,
        mesh=mesh,
        in_specs=(
            P("row", "col", None, None, None),
            matrix,
            matrix,
            P(),
            matrix,
            matrix,
            matrix,
            matrix,
            matrix,
            matrix,
            P("row", "col", None),
        ),
        out_specs=(
            matrix,
            matrix,
            matrix,
            matrix,
            matrix,
            matrix,
            P("row", "col", None),
            matrix,
        ),
        check_vma=False,
    )
```

```python
import functools

import jax
import jax.numpy as jnp
from jax import lax
from jax.experimental import pallas as pl
from jax.experimental.pallas import tpu as pltpu
from jax.sharding import PartitionSpec as P

STEPS = 2
LEARN_RATE = 0.05
BASE_RATE = 0.1
PACKET = 272
HEAD = 256
VMEM_LIMIT = 24 * 1024 * 1024
F32 = jnp.float32
BF16 = jnp.bfloat16


def dot(left, right):
    return jnp.dot(left, right, preferred_element_type=F32)


def dot_rows(left, right):
    return lax.dot_general(left, right, (((0,), (0,)), ((), ())), preferred_element_type=F32)


def silu_parts(half):
    above = 1.0 + jnp.tanh(half)
    value = half * above
    value_half = value.astype(BF16)
    above_half = above.astype(BF16)
    return value, value_half, above_half + value_half * (BF16(2.0) - above_half)


def silu_exact(half):
    above = 1.0 + jnp.tanh(half)
    value = half * above
    return value, above + value * (2.0 - above)


def sigmoid(value):
    return 0.5 * (1.0 + jnp.tanh(0.5 * value))


def split_two(value):
    high = value.astype(BF16)
    low = (value - high.astype(F32)).astype(BF16)
    return high, low


def shape(dims, dtype):
    return jax.ShapeDtypeStruct(dims, dtype)


def call(body, operands, out_shape, scratch=(), smem=(), hbm=(), flops=0):
    spaces = [pltpu.VMEM] * len(operands)
    for i in range(len(operands)):
        spaces[i] = pltpu.SMEM if i in smem else pltpu.HBM if i in hbm else pltpu.VMEM
    operands = [
        pltpu.with_memory_space_constraint(member, pltpu.HBM) if i in hbm else member
        for i, member in enumerate(operands)
    ]
    return pl.pallas_call(
        body,
        out_shape=tuple(out_shape),
        in_specs=[pl.BlockSpec(memory_space=space) for space in spaces],
        out_specs=tuple(pl.BlockSpec(memory_space=pltpu.VMEM) for _ in out_shape),
        scratch_shapes=list(scratch),
        compiler_params=pltpu.CompilerParams(vmem_limit_bytes=VMEM_LIMIT),
        cost_estimate=pl.CostEstimate(flops=flops, bytes_accessed=flops // 1000, transcendentals=0),
    )(*operands)


def start_all(pairs, semaphores):
    copies = [
        pltpu.make_async_copy(source, target, semaphores.at[i])
        for i, (source, target) in enumerate(pairs)
    ]
    for copy in copies:
        copy.start()
    return copies


def write_packet(packet_ref, one, two, rows):
    channels = one.shape[1]
    packet_ref[0:channels, :] = one.astype(BF16)
    packet_ref[channels:HEAD, :] = two.astype(BF16)
    spot = lax.broadcasted_iota(jnp.int32, (PACKET - HEAD, channels), 0)
    tail = jnp.zeros((PACKET - HEAD, channels), F32)
    for place, row in enumerate(rows):
        high, low = split_two(row)
        tail = jnp.where(spot == 2 * place, high.astype(F32), tail)
        tail = jnp.where(spot == 2 * place + 1, low.astype(F32), tail)
    packet_ref[HEAD:PACKET, :] = tail.astype(BF16)


def packet_row(tail, place):
    return tail[2 * place : 2 * place + 1, :] + tail[2 * place + 1 : 2 * place + 2, :]


def pack_body(one_hbm, two_hbm, out_hbm, packet_ref, one_ref, two_ref, out_ref, semaphores):
    pairs = [(one_hbm, one_ref), (two_hbm, two_ref), (out_hbm, out_ref)]
    for copy in start_all(pairs, semaphores):
        copy.wait()
    write_packet(packet_ref, one_ref[...], two_ref[...], [out_ref[...]])


def pack(params):
    outs = [shape((PACKET, params[0].shape[1]), BF16)] + [shape(m.shape, F32) for m in params]
    results = call(pack_body, params, outs, [pltpu.SemaphoreType.DMA((3,))], hbm=(0, 1, 2))
    return results[0], results[1:]


def dot_turned(left, right):
    return lax.dot_general(left, right, (((1,), (1,)), ((), ())), preferred_element_type=F32)


def unpack(packet_ref):
    channels = packet_ref.shape[1]
    tail = packet_ref[HEAD:PACKET, :].astype(F32)
    return packet_ref[0:channels, :], packet_ref[channels:HEAD, :], tail[0:1, :] + tail[1:2, :]


def both(left, right):
    blank = jnp.zeros_like(left)
    return jnp.concatenate(
        [jnp.concatenate([left, blank], axis=1), jnp.concatenate([blank, right], axis=1)], axis=0
    )


OFFSET = 2


def judge_steps(pair, result):
    images, one, two, out_row, shared = pair
    half = BF16(0.5)
    one_first = jnp.concatenate(one, axis=1) if shared else both(*one)
    halves = dot(images, one_first * half)
    yield
    _, first_half, slope_first = silu_parts(halves)
    image_half = 0.5 * images.astype(F32)
    if shared:
        image_half = twice(image_half)
    product = dot(first_half, both(*two) * half)
    yield
    feature, slope_out = silu_exact(image_half + product)
    sums = jnp.sum(feature.reshape(-1, 8, feature.shape[1]), axis=0)
    sums = jnp.sum(sums, axis=0, keepdims=True)
    outer = (0.5 * out_row) * slope_out
    outer_half = outer.astype(BF16)
    product = dot_turned(outer_half, both(*two) * half)
    yield
    inner_half = product.astype(BF16) * slope_first
    channels = inner_half.shape[1] // 2
    sides = [slice(0, channels), slice(channels, 2 * channels)]
    square = dot_rows(first_half, outer_half)
    grad_two = [square[s, s] for s in sides]
    yield
    result.append((outer_half, inner_half))
    wide = dot_rows(images, inner_half)
    grad_one = [wide[:, s] if shared else wide[s, s] for s in sides]
    for i, s in enumerate(sides):
        result.append((grad_one[i], grad_two[i], sums[:, s]))


def judge_pairs(pairs):
    results = [[] for _ in pairs]
    works = [judge_steps(pair, result) for pair, result in zip(pairs, results)]
    beat = 0
    left = set(range(len(works)))
    while left:
        for place in sorted(left):
            if beat >= place * OFFSET and next(works[place], True):
                left.discard(place)
        beat += 1
    return results


def verdict_lines(triples, out_rows, signs, places, lines_ref):
    lines_ref[...] = jnp.zeros_like(lines_ref)
    spot = lax.broadcasted_iota(jnp.int32, lines_ref.shape, 0)
    outs = jnp.zeros(lines_ref.shape, F32)
    is_fake = jnp.zeros(lines_ref.shape, jnp.bool_)
    for member, (triple, out_row) in enumerate(zip(triples, out_rows)):
        lines_ref[member : member + 1, :] = triple[2]
        outs = jnp.where(spot == member, out_row, outs)
        if signs[member]:
            is_fake = is_fake | (spot == member)
    features = lines_ref[...]
    scale = 1.0 / places
    verdicts = jnp.sum(features * outs, axis=1, keepdims=True) * scale
    verdicts = jnp.broadcast_to(verdicts, features.shape)
    plus = sigmoid(verdicts) * scale
    minus = -sigmoid(-verdicts) * scale
    return verdicts, minus, jnp.where(is_fake, plus, minus)


def weigh(triples, slopes):
    totals = None
    for triple, slope in zip(triples, slopes):
        parts = [slope * member for member in triple]
        totals = parts if totals is None else [x + y for x, y in zip(totals, parts)]
    return totals


def own_grads(triples, signs, out_row, places, grads_ref, lines_ref):
    channels = out_row.shape[1]
    count = len(signs)
    verdicts, minus, slopes = verdict_lines(triples, [out_row] * count, signs, places, lines_ref)
    total_one, total_two, total_out = weigh(triples, [slopes[i : i + 1, :] for i in range(count)])
    grads_ref[0:channels, :] = total_one
    grads_ref[channels:HEAD, :] = total_two
    grads_ref[HEAD : HEAD + 8, :] = verdicts
    grads_ref[HEAD + 8 : PACKET, :] = jnp.broadcast_to(total_out, (8, channels))
    return minus


def judge_own_body(
    step, batch, reals, packet_ref, fakes_ref, reals_ref, _, grads_ref, outer_ref, inner_ref, slope_ref, lines_ref
):
    rows, channels = fakes_ref.shape
    places = rows // batch
    one, two, out_row = unpack(packet_ref)
    pairs = []
    for member in range(batch):
        span = slice(member * places, (member + 1) * places)
        images = jnp.concatenate([fakes_ref[span, :], reals_ref[step * reals + member]], axis=1)
        pairs.append((images, (one, one), (two, two), twice(out_row), False))
    results = judge_pairs(pairs)
    for member, result in enumerate(results):
        side = slice(member * channels, (member + 1) * channels)
        outer_ref[:, side] = result[0][0][:, 0:channels]
        inner_ref[:, side] = result[0][1][:, 0:channels]
    triples = [result[1] for result in results] + [result[2] for result in results]
    signs = [1] * batch + [0] * reals
    slope_ref[...] = own_grads(triples, signs, out_row, places, grads_ref, lines_ref)


def judge_fakes_body(batch, packet_ref, fakes_ref, grads_ref, outer_ref, inner_ref, slope_ref, lines_ref):
    rows, channels = fakes_ref.shape
    places = rows // batch
    one, two, out_row = unpack(packet_ref)
    images = jnp.concatenate([fakes_ref[0:places, :], fakes_ref[places:rows, :]], axis=1)
    ((terms, *triples),) = judge_pairs([(images, (one, one), (two, two), twice(out_row), False)])
    outer_ref[...], inner_ref[...] = terms
    slope_ref[...] = own_grads(triples, [1] * batch, out_row, places, grads_ref, lines_ref)


def judge_reals_body(step, reals, packet_ref, reals_ref, _, grads_ref, lines_ref):
    places = reals_ref.shape[1]
    one, two, out_row = unpack(packet_ref)
    images = jnp.concatenate([reals_ref[step * reals], reals_ref[step * reals + 1]], axis=1)
    ((_, *triples),) = judge_pairs([(images, (one, one), (two, two), twice(out_row), False)])
    own_grads(triples, [0] * reals, out_row, places, grads_ref, lines_ref)


def own_shapes(rows, channels, batch):
    wide = (rows // batch, batch * channels)
    return [shape((PACKET, channels), F32), shape(wide, BF16), shape(wide, BF16), shape((8, channels), F32)]


def judge_own(packet, fakes, reals_rows, after, step, batch, reals):
    rows, channels = fakes.shape
    body = functools.partial(judge_own_body, step, batch, reals)
    flops = 4 * 6 * 2 * 1024 * 128 * 128
    scratch = [pltpu.VMEM((8, channels), F32)]
    operands = [packet, fakes, reals_rows, after]
    return call(body, operands, own_shapes(rows, channels, batch), scratch, flops=flops)


def judge_fakes(packet, fakes, batch):
    rows, channels = fakes.shape
    body = functools.partial(judge_fakes_body, batch)
    flops = 2 * 6 * 2 * 1024 * 128 * 128
    scratch = [pltpu.VMEM((8, channels), F32)]
    return call(body, [packet, fakes], own_shapes(rows, channels, batch), scratch, flops=flops)


def judge_reals(packet, reals_rows, after, step, reals):
    channels = packet.shape[1]
    body = functools.partial(judge_reals_body, step, reals)
    flops = 2 * 6 * 2 * 1024 * 128 * 128
    scratch = [pltpu.VMEM((8, channels), F32)]
    return call(body, [packet, reals_rows, after], [shape((PACKET, channels), F32)], scratch, flops=flops)[0]


def judge_others_body(judges, batch, *refs):
    refs = list(refs)
    packets = [refs.pop(0) for _ in range(judges)]
    fakes_ref = refs.pop(0)
    refs.pop(0)
    grads = [refs.pop(0) for _ in range(judges)]
    terms = [(refs.pop(0), refs.pop(0)) for _ in range(judges * batch // 2)]
    slope_ref = refs.pop(0)
    lines_ref = refs.pop(0)
    rows, channels = fakes_ref.shape
    places = rows // batch
    parts = [unpack(packet) for packet in packets]
    spans = [slice(member * places, (member + 1) * places) for member in range(batch)]
    pairs = []
    homes = []
    for which in range(0, judges, 2):
        ones, twos, outs = zip(*parts[which : which + 2])
        for member, span in enumerate(spans):
            pairs.append((fakes_ref[span, :], ones, twos, jnp.concatenate(outs, axis=1), True))
            homes.append(((which, member), (which + 1, member)))
    found = {}
    for result, home, (outer_ref, inner_ref) in zip(judge_pairs(pairs), homes, terms):
        outer_ref[...], inner_ref[...] = result[0]
        for side, key in enumerate(home):
            found[key] = result[1 + side]
    keys = sorted(found)
    triples = [found[key] for key in keys]
    out_rows = [parts[which][2] for which, _ in keys]
    verdicts, minus, slopes = verdict_lines(triples, out_rows, [1] * len(triples), places, lines_ref)
    slope_ref[...] = minus
    for which in range(judges):
        mine = range(which * batch, (which + 1) * batch)
        totals = weigh([triples[i] for i in mine], [slopes[i : i + 1, :] for i in mine])
        tail = [totals[2]] + [verdicts[i : i + 1, :] for i in mine]
        write_packet(grads[which], totals[0], totals[1], tail)


def judge_others(packets, fakes, batch, after):
    rows, channels = fakes.shape
    judges = len(packets)
    outs = [shape((PACKET, channels), BF16)] * judges
    outs = outs + [shape((rows // batch, 2 * channels), BF16)] * (judges * batch)
    outs = outs + [shape((8, channels), F32)]
    body = functools.partial(judge_others_body, judges, batch)
    scratch = [pltpu.VMEM((8, channels), F32)]
    flops = 2 * judges * 6 * 2 * 1024 * 128 * 128
    results = call(body, list(packets) + [fakes, after], outs, scratch, flops=flops)
    return results[:judges], results[judges:-1], results[-1]


def twice(tile):
    return jnp.concatenate([tile, tile], axis=1)


def gen_forward(latent, w_in, base, w_one, w_two, outs):
    fakes_ref, hidden_ref, middle_ref, gen_slope_ref, mid_slope_ref = outs
    places, channels = base.shape
    shifted = 0.5 * dot(latent.astype(BF16), w_in.astype(BF16))
    shift_row = jnp.concatenate([shifted[0:1, :], shifted[1:2, :]], axis=1)
    one = w_one.astype(BF16) * BF16(0.5)
    two = w_two.astype(BF16)
    _, hidden_half, slope_gen = silu_parts(twice(0.5 * base.astype(BF16).astype(F32)) + shift_row)
    _, middle_half, slope_mid = silu_parts(dot(hidden_half, both(one, one)))
    fakes = (hidden_half.astype(F32) + dot(middle_half, both(two, two))).astype(BF16)
    fakes_ref[0:places, :] = fakes[:, 0:channels]
    fakes_ref[places : 2 * places, :] = fakes[:, channels : 2 * channels]
    hidden_ref[...] = hidden_half
    middle_ref[...] = middle_half
    gen_slope_ref[...] = slope_gen
    mid_slope_ref[...] = slope_mid


def stored_shapes(places, channels):
    wide = (places, 2 * channels)
    return [
        shape((2 * places, channels), BF16),
        shape(wide, BF16),
        shape(wide, BF16),
        shape(wide, BF16),
        shape(wide, BF16),
    ]


def begin_body(batch, reals, seed_hbm, index_hbm, *refs):
    bank, data, *weights = refs[:6]
    weight_refs = refs[6:10]
    latent_ref, reals_ref = refs[10:12]
    outs = refs[12:17]
    bank_ref, seed_ref, index_ref, semaphores = refs[17:]
    count = len(weights) + 3
    pairs = [(seed_hbm, seed_ref), (index_hbm, index_ref), (bank, bank_ref)]
    copies = start_all(pairs + list(zip(weights, weight_refs)), semaphores)
    latent_ref[...] = jnp.zeros_like(latent_ref)
    for copy in copies[:2]:
        copy.wait()
    late = []
    for step in range(STEPS):
        for member in range(reals):
            late.append((data.at[index_ref[step, member]], reals_ref.at[step * reals + member]))
    late = start_all(late, semaphores.at[pl.ds(count, len(late))])
    for copy in copies[2:]:
        copy.wait()
    for step in range(STEPS):
        for member in range(batch):
            row = bank_ref[pl.ds(seed_ref[step, member], 1), :]
            latent_ref[step, member : member + 1, :] = row.astype(BF16).astype(F32)
    w_in, base, w_one, w_two = [ref[...] for ref in weight_refs]
    gen_forward(latent_ref[0], w_in, base, w_one, w_two, outs)
    for copy in late:
        copy.wait()


def begin(seed, index, bank, data, weights):
    batch = seed.shape[1]
    reals = index.shape[1]
    places, channels = weights[1].shape
    outs = [shape(member.shape, F32) for member in weights]
    outs = outs + [shape((STEPS, 8, channels), F32), shape((STEPS * reals, places, channels), BF16)]
    outs = outs + stored_shapes(places, channels)
    scratch = [
        pltpu.VMEM(bank.shape, F32),
        pltpu.SMEM(seed.shape, jnp.int32),
        pltpu.SMEM(index.shape, jnp.int32),
        pltpu.SemaphoreType.DMA((len(weights) + 3 + STEPS * reals,)),
    ]
    operands = [seed, index, bank, data] + list(weights)
    body = functools.partial(begin_body, batch, reals)
    flops = 4 * 2 * 1024 * 128 * 128
    results = call(body, operands, outs, scratch, hbm=range(8), flops=flops)
    return results[:4], results[4], results[5], results[6:]


def gen_back_body(step, judges, batch, *refs):
    is_last = step == STEPS - 1
    refs = list(refs)
    packets = [refs.pop(0) for _ in range(1 + judges)]
    own_terms = [refs.pop(0) for _ in range(2)]
    terms = [(refs.pop(0), refs.pop(0)) for _ in range(judges * batch // 2)]
    own_slope, slope_ref = [refs.pop(0) for _ in range(2)]
    hidden_ref, middle_ref, gen_slope_ref, mid_slope_ref, latent_ref = [refs.pop(0) for _ in range(5)]
    in_ref, base_ref, one_ref, two_ref = [refs.pop(0) for _ in range(4)]
    new_in, new_base, new_one, new_two = [refs.pop(0) for _ in range(4)]
    places, channels = base_ref.shape
    sides = (slice(0, channels), slice(channels, 2 * channels))

    def weighed(pair, ones, lines):
        outer, inner = pair
        unit = outer[...].astype(F32) + dot_turned(inner[...], both(*ones))
        return unit * jnp.concatenate(lines, axis=1)

    ones = [packet[0:channels, :] for packet in packets]
    own_lines = [own_slope[member : member + 1, :] for member in range(batch)]
    cotangent = weighed(own_terms, (ones[0], ones[0]), own_lines)
    halves = [None] * batch
    places_left = iter(terms)
    for which in range(0, judges, 2):
        for member in range(batch):
            lines = []
            for judge in (which, which + 1):
                place = judge * batch + member
                lines.append(slope_ref[place : place + 1, :])
            part = weighed(next(places_left), (ones[1 + which], ones[2 + which]), lines)
            part = part[:, sides[0]] + part[:, sides[1]]
            halves[member] = part if halves[member] is None else halves[member] + part
    cotangent = cotangent + jnp.concatenate(halves, axis=1)
    cotangent_half = cotangent.astype(BF16)
    one = one_ref[...].astype(BF16)
    two = two_ref[...].astype(BF16) * BF16(0.5)
    inner_half = (dot_turned(cotangent_half, both(two, two)).astype(BF16) * mid_slope_ref[...])
    outer = (cotangent + dot_turned(inner_half, both(one, one))) * gen_slope_ref[...].astype(F32)
    square_two = dot_rows(middle_ref[...], cotangent_half)
    square_one = dot_rows(hidden_ref[...], inner_half)
    grad_two = [square_two[side, side] for side in sides]
    grad_one = [square_one[side, side] for side in sides]
    sums = jnp.sum(jnp.sum(outer.reshape(-1, 8, 2 * channels), axis=0), axis=0, keepdims=True)
    latent_turned = latent_ref[step].T
    grad_in = [
        latent_turned[:, member : member + 1] * (0.5 * sums[:, side])
        for member, side in enumerate(sides)
    ]
    base = base_ref[...] - (0.5 * BASE_RATE * places) * (outer[:, sides[0]] + outer[:, sides[1]])
    w_one = one_ref[...] - LEARN_RATE * (grad_one[0] + grad_one[1])
    w_two = two_ref[...] - LEARN_RATE * (grad_two[0] + grad_two[1])
    w_in = in_ref[...] - LEARN_RATE * (grad_in[0] + grad_in[1])
    new_in[...] = w_in
    new_base[...] = base
    new_one[...] = w_one
    new_two[...] = w_two
    if not is_last:
        gen_forward(latent_ref[step + 1], w_in, base, w_one, w_two, refs)


def gen_back(step, packets, own_terms, terms, slopes, stored, latents, weights):
    places, channels = weights[1].shape
    batch = stored[0].shape[0] // places
    operands = list(packets) + list(own_terms) + list(terms) + list(slopes)
    operands = operands + list(stored[1:]) + [latents] + list(weights)
    outs = [shape(member.shape, F32) for member in weights]
    if step < STEPS - 1:
        outs = outs + stored_shapes(places, channels)
    body = functools.partial(gen_back_body, step, len(packets) - 1, batch)
    flops = 24 * 2 * 1024 * 128 * 128
    results = call(body, operands, outs, flops=flops)
    return results[:4], results[4:]


def disc_update_body(batch, reals, is_last, *refs):
    refs = list(refs)
    grads_ref = refs.pop(0)
    reals_ref = None if is_last else refs.pop(0)
    returns = [refs.pop(0) for _ in range(4)]
    refs.pop(0)
    params = [refs.pop(0) for _ in range(3)]
    before = refs.pop(0) if is_last else None
    news = [refs.pop(0) for _ in range(3)]
    last_ref = refs.pop(0)
    channels = params[0].shape[0]
    one = grads_ref[0:channels, :]
    two = grads_ref[channels:HEAD, :]
    out = grads_ref[HEAD + 8 : HEAD + 9, :]
    verdicts = [grads_ref[HEAD + i : HEAD + 1 + i, :] for i in range(batch + reals)]
    if reals_ref is not None:
        one = one + reals_ref[0:channels, :]
        two = two + reals_ref[channels:HEAD, :]
        out = out + reals_ref[HEAD + 8 : HEAD + 9, :]
        verdicts[batch:] = [reals_ref[HEAD + i : HEAD + 1 + i, :] for i in range(reals)]
    tails = []
    for back in returns:
        one = one + back[0:channels, :].astype(F32)
        two = two + back[channels:HEAD, :].astype(F32)
        tail = back[HEAD:PACKET, :].astype(F32)
        out = out + packet_row(tail, 0)
        tails.append([packet_row(tail, 1 + i) for i in range(batch)])
    ordered = verdicts[:batch]
    for axis, (inner, outer) in (("row", (tails[2], tails[1])), ("col", (tails[3], tails[0]))):
        is_odd = lax.rem(lax.axis_index(axis), 2) == 1
        ordered = ordered + [jnp.where(is_odd, a, b) for a, b in zip(inner, outer)]
        ordered = ordered + [jnp.where(is_odd, b, a) for a, b in zip(inner, outer)]
    ordered = ordered + verdicts[batch:]
    updated = [member[...] - LEARN_RATE * grad for member, grad in zip(params, (one, two, out))]
    for new, value in zip(news, updated):
        new[...] = value
    lanes = lax.broadcasted_iota(jnp.int32, (1, channels), 1)
    line = jnp.zeros((1, channels), F32)
    for place, value in enumerate(ordered):
        line = jnp.where(lanes == place, value, line)
    count = len(ordered)
    if is_last:
        last_ref[0:1, :] = before[0:1, 0:count]
        last_ref[1:2, :] = line[:, 0:count]
    else:
        last_ref[...] = line
        write_packet(refs[0], updated[0], updated[1], [updated[2]])


def disc_update(grads, returns, after, params, before, batch, reals):
    is_last = before is not None
    operands = list(grads) + list(returns) + [after] + list(params) + ([before] if is_last else [])
    outs = [shape(member.shape, F32) for member in params]
    if is_last:
        outs = outs + [shape((STEPS, 5 * batch + reals), F32)]
    else:
        outs = outs + [shape((1, 128), F32), shape((PACKET, 128), BF16)]
    body = functools.partial(disc_update_body, batch, reals, is_last)
    return call(body, operands, outs, hbm=(5,) if is_last else ())


def paired(block, axis, offset):
    count = lax.axis_size(axis)
    route = []
    for i in range(0, count, 2):
        first, second = (i + offset) % count, (i + offset + 1) % count
        route += [(first, second), (second, first)]
    return lax.ppermute(block, axis, route)


EDGES = (("col", 1), ("row", 1), ("row", 0), ("col", 0))


def on_device(
    data, real_index, latent_seed, latent_bank, g_in, g_base, g_one, g_two, d_one, d_two, d_out
):
    batch = latent_seed.shape[3]
    reals = real_index.shape[3]
    packet, discs = pack([d_one[0, 0], d_two[0, 0], d_out[0]])
    verdict = None
    for step in range(STEPS):
        is_last = step == STEPS - 1
        arrived = [paired(packet, axis, offset) for axis, offset in EDGES]
        if step == 0:
            gens, latents, reals_rows, stored = begin(
                latent_seed[0, 0],
                real_index[0, 0],
                latent_bank,
                data[0, 0],
                [member[0, 0] for member in (g_in, g_base, g_one, g_two)],
            )
        fakes = stored[0]
        if step == 0:
            own, *own_terms, own_slope = judge_fakes(packet, fakes, batch)
        else:
            own, *own_terms, own_slope = judge_own(packet, fakes, reals_rows, stored[1], step, batch, reals)
        arrived = arrived[::-1]
        grads, terms, slope = judge_others(arrived, fakes, batch, own_slope)
        returns = [paired(grad, *edge) for grad, edge in zip(grads[::-1], EDGES)]
        gens, stored = gen_back(
            step, [packet] + arrived, own_terms, terms, [own_slope, slope], stored, latents, gens
        )
        own = [own] if step else [own, judge_reals(packet, reals_rows, slope, step, reals)]
        results = disc_update(
            own, returns, gens[0], discs, verdict if is_last else None, batch, reals
        )
        discs = results[:3]
        verdict = results[3]
        packet = None if is_last else results[4]
    finals = [member[None, None] for member in gens] + [
        discs[0][None, None],
        discs[1][None, None],
        discs[2][None],
        verdict[None, None],
    ]
    return tuple(finals)


def solution(mesh):
    matrix = P("row", "col", None, None)
    return jax.shard_map(
        on_device,
        mesh=mesh,
        in_specs=(
            P("row", "col", None, None, None),
            matrix,
            matrix,
            P(),
            matrix,
            matrix,
            matrix,
            matrix,
            matrix,
            matrix,
            P("row", "col", None),
        ),
        out_specs=(
            matrix,
            matrix,
            matrix,
            matrix,
            matrix,
            matrix,
            P("row", "col", None),
            matrix,
        ),
        check_vma=False,
    )
```
